32 devices in a mesh: ctx: 16 (over z, x, core), tp: 2 (over y).
Axes of the slice: x: 2, y: 2, z: 4, core: 2. Of those that a mesh axis runs over, the one named last changes fastest.
Arguments:
- inputs: bfloat16 [8192, 5376], P('ctx', 'tp')
- in_gain: float32 [5376], replicated, may hold values from 0.1 to 1.9
- q_weight: bfloat16 [5376, 4096], P('ctx', 'tp')
- key_matrix: bfloat16 [5376, 2048], P('ctx', 'tp')
- value_matrix: bfloat16 [5376, 2048], P('ctx', 'tp'), may hold values from -0.078125 to 0.078125
- q_gain: float32 [128], replicated
- key_norm_gain: float32 [128], replicated
- out_weight: bfloat16 [4096, 5376], P('tp', 'ctx')
- post_gain: float32 [5376], P('tp'), may hold values from 0.1 to 1.9
- segment_ids: int32 [8192], P('ctx'), may hold values from 0 to 10, as said below
- positions: int32 [8192], P('ctx'), may hold values from 0 to 1535, as said below
Outputs:
- outputs: bfloat16 [8192, 5376], P('ctx', 'tp')
The draws below stay inside these ranges and needn't reach their ends.
Inputs may be any that keep to these rules, and one draw needn't show every extreme that they name: segment_ids start at 0 and rise by 0 or 1 from each token to the next. positions are 0 at the first token of each document and rise by 1 within it; no document has more than 1536 tokens, and the last document has exactly 1536.
All inputs are finite; a program needn't handle non-finite values.
Results may differ from the reference program's by a relative error of at most 0.013.
The reference program's roundings to bfloat16 on the way count: a program that leaves them out, or rounds other values in their place, can miss the bound.
Values may be sent and summed in bfloat16 or wider, within the bound.
No kernel may reach another device: no remote copies, remote signals or barrier semaphores. Data moves between devices by JAX's collectives and lax.ppermute only.
A program may use at most 192 MiB of HBM per device.

```python
import math
import jax
import jax.numpy as jnp
from jax import lax

MODEL_WIDTH = 5376
QUERY_HEADS = 32
KEY_HEADS = 16
HEAD_SIZE = 128
VISIBLE_SPAN = 1024
SLAB_TOKENS = 8192
N_TP = 2


def document_helper(key):
    cell_size = VISIBLE_SPAN // 2
    cell_count = SLAB_TOKENS // cell_size
    free_cells = cell_count - 3
    skip_total = free_cells // 2 // 2
    cell = jnp.arange(cell_count, dtype=jnp.int32)
    offsets = jax.random.randint(jax.random.fold_in(key, 7), (cell_count,), 0, cell_size).astype(jnp.int32)
    offsets = jnp.where(cell == 0, 0, offsets).astype(jnp.int32)
    candidate = (cell % 2 == 1) & (cell < free_cells)
    ranking = jax.random.randint(jax.random.fold_in(key, 9), (cell_count,), 0, 65536).astype(jnp.int32) * cell_count + cell
    ranking = jnp.where(candidate, ranking, 65536 * cell_count + cell_count).astype(jnp.int32)
    order = jnp.argsort(ranking, stable=True).astype(jnp.int32)
    rank = jnp.argsort(order, stable=True).astype(jnp.int32)
    skipped = candidate & (rank < skip_total)
    has_start = ((cell < free_cells) & jnp.logical_not(skipped)).astype(jnp.int32)
    begin_points = cell * cell_size + offsets
    index = jnp.arange(SLAB_TOKENS, dtype=jnp.int32)
    starts = jnp.zeros((SLAB_TOKENS,), jnp.int32).at[begin_points].max(has_start)
    starts = starts.at[free_cells * cell_size].set(1)
    segments = jnp.cumsum(starts) - 1
    begins = lax.cummax(jnp.where(starts > 0, index, 0))
    return (segments.astype(jnp.int32), (index - begins).astype(jnp.int32))


def draw_segment_ids(key, part):
    return document_helper(key)[0]


def draw_positions(key, part):
    return document_helper(key)[1]


def draw_inputs(key, part):
    base = jnp.clip(jax.random.normal(jax.random.fold_in(key, 41), (SLAB_TOKENS, MODEL_WIDTH), jnp.float32), -6.0, 6.0)
    return base.astype(jnp.bfloat16)


def projection_helper(key):
    head_group = QUERY_HEADS // KEY_HEADS
    query_offset = jax.random.normal(jax.random.fold_in(key, 23), (MODEL_WIDTH, KEY_HEADS, head_group, HEAD_SIZE), jnp.float32) * MODEL_WIDTH ** (-0.5)
    key_offset = jax.random.normal(jax.random.fold_in(key, 29), (MODEL_WIDTH, KEY_HEADS, HEAD_SIZE), jnp.float32) * MODEL_WIDTH ** (-0.5)
    return (query_offset.reshape(MODEL_WIDTH, QUERY_HEADS * HEAD_SIZE), key_offset.reshape(MODEL_WIDTH, KEY_HEADS * HEAD_SIZE))


def draw_q_weight(key, part):
    return projection_helper(key)[0].astype(jnp.bfloat16)


def draw_key_matrix(key, part):
    return projection_helper(key)[1].astype(jnp.bfloat16)


def gain_helper(key, salt):
    return jax.random.uniform(jax.random.fold_in(key, salt), (HEAD_SIZE,), jnp.float32, 0.8, 1.6)


def draw_q_gain(key, part):
    return gain_helper(key, 11)


def draw_key_norm_gain(key, part):
    return gain_helper(key, 13)


def draw_out_weight(key, part):
    rows = QUERY_HEADS * HEAD_SIZE
    base = jax.random.normal(jax.random.fold_in(key, 17), (rows, MODEL_WIDTH), jnp.float32) * rows ** (-0.5)
    column = jnp.arange(MODEL_WIDTH, dtype=jnp.float32) / MODEL_WIDTH
    jitter = jax.random.uniform(jax.random.fold_in(key, 19), (MODEL_WIDTH,), jnp.float32, 0.7, 1.3)
    scale = 10.0 ** column * jitter
    return (base * scale[None, :]).astype(jnp.bfloat16)


def steps_of(rng, shape, cuts, low, largest):
    loudness, own = 1.0, jax.random.fold_in(rng, 6)
    for dim, blocks in cuts:
        heights = jnp.exp(jax.random.uniform(jax.random.fold_in(own, dim), (blocks,), jnp.float32, low / len(cuts), largest / len(cuts)))
        loudness = loudness * jnp.repeat(heights, shape[dim] // blocks).reshape([-1 if axis == dim else 1 for axis in range(len(shape))])
    return loudness


def bell_draw(key, dims, width, reach, split=(), kind=jnp.bfloat16):
    entries = width * jax.random.normal(key, dims, jnp.float32)
    if split:
        entries = entries * steps_of(key, dims, split, -0.22, 0.18)
    return jnp.clip(entries, -reach, reach).astype(kind)


def setup_inputs(seed: int = 0) -> dict:
    key_of = jax.random.split(jax.random.key(seed), 12)
    inputs = draw_inputs(jax.random.fold_in(key_of[11], 71), 0)
    in_gain = jnp.clip(1.0 + 0.18 * jax.random.normal(key_of[1], (MODEL_WIDTH,), jnp.float32), 0.1, 1.9)
    q_weight = draw_q_weight(jax.random.fold_in(key_of[11], 71), 0)
    key_matrix = draw_key_matrix(jax.random.fold_in(key_of[11], 71), 0)
    value_matrix = bell_draw(key_of[4], (MODEL_WIDTH, KEY_HEADS * HEAD_SIZE), MODEL_WIDTH ** -0.5, 0.078125, ((0, 16), (1, 2)))
    q_gain = draw_q_gain(jax.random.fold_in(key_of[11], 71), 0)
    key_norm_gain = draw_key_norm_gain(jax.random.fold_in(key_of[11], 71), 0)
    out_weight = draw_out_weight(jax.random.fold_in(key_of[11], 71), 0)
    post_gain = jnp.clip(1.0 + 0.18 * jax.random.normal(key_of[8], (MODEL_WIDTH,), jnp.float32), 0.1, 1.9)
    segment_ids = draw_segment_ids(jax.random.fold_in(key_of[11], 71), 0)
    positions = draw_positions(jax.random.fold_in(key_of[11], 71), 0)
    return dict(inputs=inputs, in_gain=in_gain, q_weight=q_weight, key_matrix=key_matrix, value_matrix=value_matrix, q_gain=q_gain, key_norm_gain=key_norm_gain, out_weight=out_weight, post_gain=post_gain, segment_ids=segment_ids, positions=positions)


EPS = 1e-06
ROPE_BASE = 10000.0
MASKED = -1e+30

def rms_scale(values, gain):
    return values * lax.rsqrt(lax.optimization_barrier(jnp.mean(values * values, axis=-1, keepdims=True)) + EPS) * gain

def rotate(values, position):
    half_dim = values.shape[-1] // 2
    frequency = ROPE_BASE ** (-jnp.arange(half_dim, dtype=jnp.float32) / half_dim)
    angles = position.astype(jnp.float32)[:, None] * frequency[None, :]
    cosine = jnp.cos(angles)[:, None, :]
    sine = jnp.sin(angles)[:, None, :]
    first = values[..., :half_dim]
    second = values[..., half_dim:]
    return jnp.concatenate([first * cosine - second * sine, second * cosine + first * sine], axis=-1)

def prepare_heads(projected, gain, position, heads, factor):
    shaped = projected.reshape(projected.shape[0], heads, HEAD_SIZE)
    return (rotate(rms_scale(shaped, gain), position) * factor).astype(jnp.bfloat16)

def reference(inputs, in_gain, q_weight, key_matrix, value_matrix, q_gain, key_norm_gain, out_weight, post_gain, segment_ids, positions):
    source = inputs.astype(jnp.float32)
    normalized = rms_scale(source, in_gain).astype(jnp.bfloat16)
    query_heads_all = prepare_heads(jnp.dot(normalized, q_weight, preferred_element_type=jnp.float32), q_gain, positions, QUERY_HEADS, (MODEL_WIDTH // QUERY_HEADS) ** (-0.5))
    every_key = prepare_heads(jnp.dot(normalized, key_matrix, preferred_element_type=jnp.float32), key_norm_gain, positions, KEY_HEADS, 1.0)
    every_value = jnp.dot(normalized, value_matrix, preferred_element_type=jnp.float32).reshape(SLAB_TOKENS, KEY_HEADS, HEAD_SIZE).astype(jnp.bfloat16)
    block_of_queries = math.gcd(SLAB_TOKENS, 512)
    span = VISIBLE_SPAN + block_of_queries
    head_group = QUERY_HEADS // KEY_HEADS
    padded_keys = jnp.concatenate([jnp.zeros((VISIBLE_SPAN, KEY_HEADS, HEAD_SIZE), jnp.bfloat16), every_key], axis=0)
    padded_values = jnp.concatenate([jnp.zeros((VISIBLE_SPAN, KEY_HEADS, HEAD_SIZE), jnp.bfloat16), every_value], axis=0)
    segment_pad = jnp.concatenate([jnp.full((VISIBLE_SPAN,), -1, jnp.int32), segment_ids.astype(jnp.int32)], axis=0)

    def one_block(block):
        start_token = (block * block_of_queries).astype(jnp.int32)
        rows_of_queries = lax.dynamic_slice_in_dim(query_heads_all, start_token, block_of_queries, 0).reshape(block_of_queries, KEY_HEADS, head_group, HEAD_SIZE)
        key_rows = lax.dynamic_slice_in_dim(padded_keys, start_token, span, 0)
        value_rows = lax.dynamic_slice_in_dim(padded_values, start_token, span, 0)
        key_segments = lax.dynamic_slice_in_dim(segment_pad, start_token, span, 0)
        query_segments = lax.dynamic_slice_in_dim(segment_ids.astype(jnp.int32), start_token, block_of_queries, 0)
        query_index = start_token + jnp.arange(block_of_queries, dtype=jnp.int32)
        key_index = start_token - VISIBLE_SPAN + jnp.arange(span, dtype=jnp.int32)
        gap = query_index[:, None] - key_index[None, :]
        allowed = (query_segments[:, None] == key_segments[None, :]) & (gap >= 0) & (gap < VISIBLE_SPAN) & (key_index[None, :] >= 0)
        scores = jnp.einsum('qhgd,khd->hgqk', rows_of_queries.astype(jnp.float32), key_rows.astype(jnp.float32))
        scores = jnp.where(allowed[None, None], scores, MASKED)
        expo = jnp.exp(scores - lax.optimization_barrier(jnp.max(scores, axis=-1, keepdims=True)))
        weights = (expo / lax.optimization_barrier(jnp.sum(expo, axis=-1, keepdims=True))).astype(jnp.bfloat16)
        mixed = jnp.einsum('hgqk,khd->qhgd', weights.astype(jnp.float32), value_rows.astype(jnp.float32))
        return mixed.reshape(block_of_queries, QUERY_HEADS * HEAD_SIZE).astype(jnp.bfloat16)
    blocks = jnp.arange(SLAB_TOKENS // block_of_queries, dtype=jnp.int32)
    attended = lax.map(one_block, blocks).reshape(SLAB_TOKENS, QUERY_HEADS * HEAD_SIZE)
    cols = QUERY_HEADS * HEAD_SIZE // N_TP
    projected = jnp.zeros((SLAB_TOKENS, MODEL_WIDTH), jnp.float32)
    for group_index in range(N_TP):
        partial_term = jnp.dot(attended[:, group_index * cols:(group_index + 1) * cols], out_weight[group_index * cols:(group_index + 1) * cols], preferred_element_type=jnp.float32)
        projected = projected + lax.optimization_barrier(partial_term.astype(jnp.bfloat16)).astype(jnp.float32)
    return (source + rms_scale(projected, post_gain)).astype(jnp.bfloat16)
```

```python
import jax
import jax.numpy as jnp
from jax import lax
from jax.sharding import PartitionSpec as P

MODEL_WIDTH = 5376
QUERY_HEADS = 32
HEAD_SIZE = 128
VISIBLE_SPAN = 1024


EPS = 1e-06
ROPE_BASE = 10000.0
MASKED = -1e30


def from_behind(x, axis, by):
    size = lax.axis_size(axis)
    pairs = [(i, i + by) for i in range(size) if 0 <= i + by < size]
    return lax.ppermute(x, axis, pairs)


def rms_scale(values, gain):
    return values * lax.rsqrt(jnp.mean(values * values, axis=-1, keepdims=True) + EPS) * gain


def rotate(values, position):
    half_dim = values.shape[-1] // 2
    frequency = ROPE_BASE ** (-jnp.arange(half_dim, dtype=jnp.float32) / half_dim)
    angles = position.astype(jnp.float32)[:, None] * frequency[None, :]
    cosine = jnp.cos(angles)[:, None, :]
    sine = jnp.sin(angles)[:, None, :]
    first = values[..., :half_dim]
    second = values[..., half_dim:]
    return jnp.concatenate(
        [first * cosine - second * sine, second * cosine + first * sine], axis=-1
    )


def prepare_heads(projected, gain, position, heads, factor):
    shaped = projected.reshape(projected.shape[0], heads, HEAD_SIZE)
    return (rotate(rms_scale(shaped, gain), position) * factor).astype(jnp.bfloat16)


def block_scores(grouped, keys_block):
    return jnp.einsum("qhgd,khd->hgqk", grouped, keys_block, preferred_element_type=jnp.float32)


def block_mix(weights_block, values_block):
    return jnp.einsum(
        "hgqk,khd->qhgd", weights_block, values_block, preferred_element_type=jnp.float32
    )


def gather_features(inputs):
    if lax.axis_size("tp") != 2:
        return lax.all_gather(inputs, "tp", axis=1, tiled=True)
    other = lax.ppermute(inputs, "tp", [(0, 1), (1, 0)])
    first = lax.axis_index("tp") == 0
    return jnp.concatenate(
        [jnp.where(first, inputs, other), jnp.where(first, other, inputs)], axis=1
    )


def project_out(attended, out_full):
    if lax.axis_size("tp") != 2:
        partial_terms = jnp.dot(attended, out_full, preferred_element_type=jnp.float32)
        return lax.psum_scatter(
            partial_terms.astype(jnp.bfloat16), "tp", scatter_dimension=1, tiled=True
        ).astype(jnp.float32)
    here = lax.axis_index("tp")
    cols = out_full.shape[1] // 2

    def half(which):
        weight = lax.dynamic_slice_in_dim(out_full, which * cols, cols, axis=1)
        return jnp.dot(attended, weight, preferred_element_type=jnp.float32).astype(jnp.bfloat16)

    theirs = half(1 - here)
    arrived = lax.ppermute(theirs, "tp", [(0, 1), (1, 0)])
    return half(here).astype(jnp.float32) + arrived.astype(jnp.float32)


def local(
    inputs,
    in_gain,
    q_weight,
    key_matrix,
    value_matrix,
    q_gain,
    key_norm_gain,
    out_weight,
    post_gain,
    segment_ids,
    positions,
):
    tok_rows = inputs.shape[0]
    q_cols = q_weight.shape[1]
    kv_cols = key_matrix.shape[1]
    stacked = jnp.concatenate([key_matrix, value_matrix, q_weight], axis=1)
    weights_full = lax.all_gather(stacked, "ctx", axis=0, tiled=True)
    out_full = lax.all_gather(out_weight, "ctx", axis=1, tiled=True)
    gathered = gather_features(inputs)
    normalized = rms_scale(gathered.astype(jnp.float32), in_gain).astype(jnp.bfloat16)
    raw = jnp.dot(normalized, weights_full, preferred_element_type=jnp.float32)
    k_raw = raw[:, :kv_cols]
    v_raw = raw[:, kv_cols : 2 * kv_cols]
    q_raw = raw[:, 2 * kv_cols :]
    q_heads = q_cols // HEAD_SIZE
    kv_heads = kv_cols // HEAD_SIZE
    query_heads_all = prepare_heads(
        q_raw, q_gain, positions, q_heads, (MODEL_WIDTH // QUERY_HEADS) ** (-0.5)
    )
    keys_own = prepare_heads(k_raw, key_norm_gain, positions, kv_heads, 1.0)
    values_own = v_raw.reshape(tok_rows, kv_heads, HEAD_SIZE).astype(jnp.bfloat16)
    reach = (VISIBLE_SPAN - 1) // tok_rows + 1
    key_list = [keys_own]
    value_list = [values_own]
    segment_list = [segment_ids]
    for distance in range(1, reach + 1):
        far_keys, far_values, far_segments = from_behind(
            (keys_own, values_own, segment_ids), "ctx", distance
        )
        key_list.insert(0, far_keys)
        value_list.insert(0, far_values)
        segment_list.insert(0, far_segments)
    key_all = jnp.concatenate(key_list, axis=0)
    value_all = jnp.concatenate(value_list, axis=0)
    segment_all = jnp.concatenate(segment_list, axis=0)
    my_start = lax.axis_index("ctx") * tok_rows
    key_index = my_start - reach * tok_rows + jnp.arange((reach + 1) * tok_rows, dtype=jnp.int32)
    query_index = my_start + jnp.arange(tok_rows, dtype=jnp.int32)
    gap = query_index[:, None] - key_index[None, :]
    allowed = (
        (segment_ids[:, None] == segment_all[None, :])
        & (gap >= 0)
        & (gap < VISIBLE_SPAN)
        & (key_index[None, :] >= 0)
    )
    head_group = q_heads // kv_heads
    grouped = query_heads_all.reshape(tok_rows, kv_heads, head_group, HEAD_SIZE)
    scores = block_scores(grouped, key_all)
    scores = jnp.where(allowed[None, None], scores, MASKED)
    expo = jnp.exp(scores - jnp.max(scores, axis=-1, keepdims=True))
    weights = (expo / jnp.sum(expo, axis=-1, keepdims=True)).astype(jnp.bfloat16)
    mixed = block_mix(weights, value_all)
    attended = mixed.reshape(tok_rows, q_cols).astype(jnp.bfloat16)
    share = project_out(attended, out_full)
    squares = lax.psum(jnp.sum(share * share, axis=-1), "tp")
    branch = share * lax.rsqrt(squares[:, None] / MODEL_WIDTH + EPS) * post_gain
    return (inputs.astype(jnp.float32) + branch).astype(jnp.bfloat16)


def solution(mesh):
    return jax.shard_map(
        local,
        mesh=mesh,
        in_specs=(
            P("ctx", "tp"),
            P(),
            P("ctx", "tp"),
            P("ctx", "tp"),
            P("ctx", "tp"),
            P(),
            P(),
            P("tp", "ctx"),
            P("tp"),
            P("ctx"),
            P("ctx"),
        ),
        out_specs=P("ctx", "tp"),
        check_vma=False,
    )
```

```python
import functools

import jax
import jax.numpy as jnp
from jax import lax
from jax.experimental import pallas as pl
from jax.experimental.pallas import tpu as pltpu
from jax.sharding import PartitionSpec as P

MODEL_WIDTH = 5376
QUERY_HEADS = 32
HEAD_SIZE = 128
VISIBLE_SPAN = 1024


EPS = 1e-06
ROPE_BASE = 10000.0
MASKED = -1e30

INNER = 4
QUERY_BLOCK = 256


def rms_scale(values, gain):
    return values * lax.rsqrt(jnp.mean(values * values, axis=-1, keepdims=True) + EPS) * gain


def angles_of(position, half_dim):
    frequency = ROPE_BASE ** (-jnp.arange(half_dim, dtype=jnp.float32) / half_dim)
    angles = position.astype(jnp.float32)[:, None] * frequency[None, :]
    return jnp.cos(angles)[:, None, :], jnp.sin(angles)[:, None, :]


def rotate(values, cosine, sine):
    half_dim = values.shape[-1] // 2
    first = values[..., :half_dim]
    second = values[..., half_dim:]
    return jnp.concatenate(
        [first * cosine - second * sine, second * cosine + first * sine], axis=-1
    )


def prepare_heads(projected, gain, turn, factor):
    shaped = projected.reshape(projected.shape[0], -1, HEAD_SIZE)
    turned = rotate(rms_scale(shaped, gain), *turn) * factor
    return turned.astype(jnp.bfloat16).reshape(projected.shape)


def swap(x, mask):
    size = lax.axis_size("ctx")
    return lax.ppermute(x, "ctx", [(c, c ^ mask) for c in range(size)])


def swap_tp(x):
    return lax.ppermute(x, "tp", [(0, 1), (1, 0)])


def ring_step(x, by=1):
    size = lax.axis_size("ctx")
    return lax.ppermute(x, "ctx", [(c, (c + by * INNER) % size) for c in range(size)])


def after(x, *others):
    return lax.optimization_barrier((x, *others))[0]


def placed(blocks, places):
    whole = jnp.zeros((len(blocks), *blocks[0].shape), blocks[0].dtype)
    for block, place in zip(blocks, places):
        whole = lax.dynamic_update_index_in_dim(whole, block, place, 0)
    return whole


def attend_kernel(pos_ref, q_ref, k_ref, v_ref, o_ref):
    start = pl.multiple_of(pl.program_id(0) * QUERY_BLOCK, QUERY_BLOCK)
    window = VISIBLE_SPAN + QUERY_BLOCK
    keys = k_ref[pl.ds(start, window), :]
    values = v_ref[pl.ds(start, window), :]
    shape = (QUERY_BLOCK, window)
    last = lax.broadcasted_iota(jnp.int32, shape, 0) + VISIBLE_SPAN
    column = lax.broadcasted_iota(jnp.int32, shape, 1)
    first = last - jnp.minimum(pos_ref[...], VISIBLE_SPAN - 1)
    allowed = (column <= last) & (column >= first)
    for head in range(q_ref.shape[1] // HEAD_SIZE):
        span = slice(head * HEAD_SIZE, (head + 1) * HEAD_SIZE)
        scores = lax.dot_general(
            q_ref[:, span], keys, (((1,), (1,)), ((), ())), preferred_element_type=jnp.float32
        )
        scores = jnp.where(allowed, scores, MASKED)
        expo = jnp.exp(scores - jnp.max(scores, axis=-1, keepdims=True))
        weights = (expo / jnp.sum(expo, axis=-1, keepdims=True)).astype(jnp.bfloat16)
        mixed = jnp.dot(weights, values, preferred_element_type=jnp.float32)
        o_ref[:, span] = mixed.astype(jnp.bfloat16)


def attend(position, queries, keys, values):
    tokens, cols = queries.shape
    window = VISIBLE_SPAN + QUERY_BLOCK
    heads = cols // HEAD_SIZE
    return pl.pallas_call(
        attend_kernel,
        grid=(tokens // QUERY_BLOCK,),
        in_specs=[
            pl.BlockSpec((QUERY_BLOCK, 1), lambda b: (b, 0)),
            pl.BlockSpec((QUERY_BLOCK, cols), lambda b: (b, 0)),
            pl.BlockSpec(keys.shape, lambda b: (0, 0)),
            pl.BlockSpec(values.shape, lambda b: (0, 0)),
        ],
        out_specs=pl.BlockSpec((QUERY_BLOCK, cols), lambda b: (b, 0)),
        out_shape=jax.ShapeDtypeStruct((tokens, cols), jnp.bfloat16),
        compiler_params=pltpu.CompilerParams(vmem_limit_bytes=40 * 2**20),
        cost_estimate=pl.CostEstimate(
            flops=4 * tokens * window * cols,
            bytes_accessed=4 * tokens * cols + 4 * keys.shape[0] * HEAD_SIZE,
            transcendentals=heads * tokens * window,
        ),
    )(position, queries, keys, values)


def group_kernel(inner, pieces, place_ref, *refs):
    lefts, weight_ref, o_ref = refs[: inner * pieces], refs[-2], refs[-1]
    place = place_ref[0]
    depth = lefts[0].shape[1]
    total = None
    for m in range(inner):
        for piece in range(pieces):
            row = pl.multiple_of(((place ^ m) * pieces + piece) * depth, depth)
            term = jnp.dot(
                lefts[m * pieces + piece][...],
                weight_ref[pl.ds(row, depth), :],
                preferred_element_type=jnp.float32,
            )
            total = term if total is None else total + term
    o_ref[...] = total.astype(jnp.bfloat16)


def group_product(place, attended, weight):
    lefts = [piece for pieces in attended for piece in pieces]
    tokens, depth = lefts[0].shape
    rows, cols = weight.shape
    block = 512
    return pl.pallas_call(
        functools.partial(group_kernel, len(attended), len(attended[0])),
        grid=(tokens // block,),
        in_specs=[pl.BlockSpec(memory_space=pltpu.SMEM)]
        + [pl.BlockSpec((block, depth), lambda b: (b, 0)) for _ in lefts]
        + [pl.BlockSpec((rows, cols), lambda b: (0, 0))],
        out_specs=pl.BlockSpec((block, cols), lambda b: (b, 0)),
        out_shape=jax.ShapeDtypeStruct((tokens, cols), jnp.bfloat16),
        compiler_params=pltpu.CompilerParams(vmem_limit_bytes=40 * 2**20),
        cost_estimate=pl.CostEstimate(
            flops=2 * tokens * rows * cols,
            bytes_accessed=2 * (tokens * rows + rows * cols + tokens * cols),
            transcendentals=0,
        ),
    )(jnp.reshape(place, (1,)), *lefts, weight)


def plane_inputs(inputs, in_gain, place, side):
    rows = inputs.shape[0]
    half = rows // 2
    a, b = inputs[:half], inputs[half:]
    a_y, b_x = swap_tp(a), swap(b, 2)
    a_x, a_xy = swap(a, 2), swap(a_y, 2)
    b_y, b_xy = swap_tp(b), swap_tp(b_x)
    mine = {(0, 0): (a, a_y), (0, 2): (a_x, a_xy), (1, 0): (b, b_y), (1, 2): (b_x, b_xy)}
    normed = jnp.zeros((INNER * rows, 2 * inputs.shape[1]), jnp.bfloat16)
    for core in (0, 1):
        for (part, mask), (near, far) in mine.items():
            if core:
                near, far = swap(near, 1), swap(far, 1)
            low = jnp.where(side == 0, near, far)
            high = jnp.where(side == 0, far, near)
            tokens = jnp.concatenate([low, high], axis=1).astype(jnp.float32)
            block = rms_scale(tokens, in_gain).astype(jnp.bfloat16)
            row = (place ^ mask ^ core) * rows + part * half
            normed = lax.dynamic_update_slice_in_dim(normed, block, row, 0)
    return normed


def quarter(weights, which):
    cut = [
        lax.dynamic_slice_in_dim(w, which * (w.shape[1] // INNER), w.shape[1] // INNER, axis=1)
        for w in weights
    ]
    return jnp.concatenate(cut, axis=1) if len(cut) > 1 else cut[0]


def plane_rows(weights, place):
    blocks = [quarter(weights, place)]
    for mask in range(1, INNER):
        blocks.append(swap(quarter(weights, place ^ mask), mask))
    whole = placed(blocks, [place ^ mask for mask in range(INNER)])
    return whole.reshape(-1, whole.shape[-1])


def by_planes(
    inputs,
    in_gain,
    q_weight,
    key_matrix,
    value_matrix,
    q_gain,
    key_norm_gain,
    out_weight,
    post_gain,
    segment_ids,
    positions,
):
    tok_rows = inputs.shape[0]
    planes = lax.axis_size("ctx") // INNER
    me = lax.axis_index("ctx")
    place, plane = me % INNER, me // INNER
    side = lax.axis_index("tp")
    plane_tokens = INNER * tok_rows

    kv_start = plane_rows([key_matrix, value_matrix], place)
    q_start = plane_rows([q_weight], place)
    q_half = q_start.shape[1] // 2
    hops = {}

    def ring(name, block):
        hops[name] = [block]

    def hop(name, *others):
        block = hops[name][-1]
        hops[name].append(ring_step(after(block, *others) if others else block))
        return hops[name][-1]

    kv_half = kv_start.shape[1] // 2
    ring("k", kv_start[:, :kv_half])
    ring("v", kv_start[:, kv_half:])
    ring("qa", q_start[:, :q_half])
    ring("qb", q_start[:, q_half:])
    ring("o", out_weight)
    steps = planes - 1
    previous = []
    order = []
    for _ in range(steps):
        order += ["k", "v"]
    for _ in range(steps):
        order += ["qa"]
    for _ in range(steps):
        order += ["qb"]
    for _ in range(steps):
        order += ["o"]
    for name in order:
        previous.append(hop(name, *previous[-2:-1]))

    source = [(plane - d) % planes for d in range(planes)]

    def whole_rows(name):
        return placed(hops[name], source).reshape(MODEL_WIDTH, -1)

    normed = plane_inputs(inputs, in_gain, place, side)
    position_blocks = [positions] + [swap(positions, mask) for mask in range(1, INNER)]
    position = placed(position_blocks, [place ^ mask for mask in range(INNER)]).reshape(-1)
    turn = angles_of(position, HEAD_SIZE // 2)
    turn = lax.optimization_barrier(turn)

    def project(name):
        return jnp.dot(normed, whole_rows(name), preferred_element_type=jnp.float32)

    size = lax.axis_size("ctx")
    up = [(c, c + INNER) for c in range(size - INNER)]

    def with_halo(own):
        far = lax.ppermute(own[plane_tokens - VISIBLE_SPAN :], "ctx", up)
        return jnp.concatenate([far, own], axis=0)

    keys = with_halo(prepare_heads(project("k"), key_norm_gain, turn, 1.0))
    values = with_halo(project("v").astype(jnp.bfloat16))
    factor = (MODEL_WIDTH // QUERY_HEADS) ** (-0.5)
    attended = [[] for _ in range(INNER)]
    for index, name in enumerate(("qa", "qb")):
        queries = prepare_heads(project(name), q_gain, turn, factor)
        span = slice(index * HEAD_SIZE, (index + 1) * HEAD_SIZE)
        own = attend(position[:, None], queries, keys[:, span], values[:, span])
        far = swap(own, 2)
        for mask, piece in zip(range(INNER), (own, swap(own, 1), far, swap(far, 1))):
            attended[mask].append(piece)

    both = ("ctx", "tp")
    cols = out_weight.shape[1]
    per_side = planes // 2
    arrived, places = [], []
    for d in range(planes):
        term = group_product(place, attended, hops["o"][d])
        pairs, inside = [], []
        for c in range(size):
            home = ((c // INNER - d) % planes) // per_side
            pairs.append((2 * c + 1 - home, 2 * c + home))
            inside.append(2 * c + home)
        other = lax.ppermute(term, both, pairs)
        total = (term.astype(jnp.float32) + other.astype(jnp.float32)).astype(jnp.bfloat16)
        for mask in range(INNER):
            row = (place ^ mask) * tok_rows
            block = lax.dynamic_slice_in_dim(total, row, tok_rows, axis=0)
            if mask:
                block = lax.ppermute(block, both, [(n, n ^ (2 * mask)) for n in inside])
            arrived.append(block)
            places.append(source[d] * INNER + (place ^ mask))
    slots = placed(arrived, places)
    mine = lax.dynamic_slice_in_dim(slots, side * per_side * INNER, per_side * INNER, axis=0)
    share = mine.transpose(1, 0, 2).reshape(tok_rows, -1).astype(jnp.float32)
    own_squares = jnp.sum(share * share, axis=-1)
    squares = own_squares + swap_tp(own_squares)
    branch = share * lax.rsqrt(squares[:, None] / MODEL_WIDTH + EPS) * post_gain
    return (inputs.astype(jnp.float32) + branch).astype(jnp.bfloat16)


def from_behind(x, axis, by):
    size = lax.axis_size(axis)
    pairs = [(i, i + by) for i in range(size) if 0 <= i + by < size]
    return lax.ppermute(x, axis, pairs)


def block_scores(grouped, keys_block):
    return jnp.einsum("qhgd,khd->hgqk", grouped, keys_block, preferred_element_type=jnp.float32)


def block_mix(weights_block, values_block):
    return jnp.einsum(
        "hgqk,khd->qhgd", weights_block, values_block, preferred_element_type=jnp.float32
    )


def gather_features(inputs):
    if lax.axis_size("tp") != 2:
        return lax.all_gather(inputs, "tp", axis=1, tiled=True)
    other = lax.ppermute(inputs, "tp", [(0, 1), (1, 0)])
    first = lax.axis_index("tp") == 0
    return jnp.concatenate(
        [jnp.where(first, inputs, other), jnp.where(first, other, inputs)], axis=1
    )


def project_out(attended, out_full):
    if lax.axis_size("tp") != 2:
        partial_terms = jnp.dot(attended, out_full, preferred_element_type=jnp.float32)
        return lax.psum_scatter(
            partial_terms.astype(jnp.bfloat16), "tp", scatter_dimension=1, tiled=True
        ).astype(jnp.float32)
    here = lax.axis_index("tp")
    cols = out_full.shape[1] // 2

    def half(which):
        weight = lax.dynamic_slice_in_dim(out_full, which * cols, cols, axis=1)
        return jnp.dot(attended, weight, preferred_element_type=jnp.float32).astype(jnp.bfloat16)

    theirs = half(1 - here)
    arrived = lax.ppermute(theirs, "tp", [(0, 1), (1, 0)])
    return half(here).astype(jnp.float32) + arrived.astype(jnp.float32)


def by_devices(
    inputs,
    in_gain,
    q_weight,
    key_matrix,
    value_matrix,
    q_gain,
    key_norm_gain,
    out_weight,
    post_gain,
    segment_ids,
    positions,
):
    tok_rows = inputs.shape[0]
    q_cols = q_weight.shape[1]
    kv_cols = key_matrix.shape[1]
    stacked = jnp.concatenate([key_matrix, value_matrix, q_weight], axis=1)
    weights_full = lax.all_gather(stacked, "ctx", axis=0, tiled=True)
    out_full = lax.all_gather(out_weight, "ctx", axis=1, tiled=True)
    gathered = gather_features(inputs)
    normalized = rms_scale(gathered.astype(jnp.float32), in_gain).astype(jnp.bfloat16)
    raw = jnp.dot(normalized, weights_full, preferred_element_type=jnp.float32)
    k_raw = raw[:, :kv_cols]
    v_raw = raw[:, kv_cols : 2 * kv_cols]
    q_raw = raw[:, 2 * kv_cols :]
    q_heads = q_cols // HEAD_SIZE
    kv_heads = kv_cols // HEAD_SIZE
    turn = angles_of(positions, HEAD_SIZE // 2)
    query_heads_all = prepare_heads(
        q_raw, q_gain, turn, (MODEL_WIDTH // QUERY_HEADS) ** (-0.5)
    )
    keys_own = prepare_heads(k_raw, key_norm_gain, turn, 1.0)
    keys_own = keys_own.reshape(tok_rows, kv_heads, HEAD_SIZE)
    values_own = v_raw.reshape(tok_rows, kv_heads, HEAD_SIZE).astype(jnp.bfloat16)
    reach = (VISIBLE_SPAN - 1) // tok_rows + 1
    key_list = [keys_own]
    value_list = [values_own]
    segment_list = [segment_ids]
    for distance in range(1, reach + 1):
        far_keys, far_values, far_segments = from_behind(
            (keys_own, values_own, segment_ids), "ctx", distance
        )
        key_list.insert(0, far_keys)
        value_list.insert(0, far_values)
        segment_list.insert(0, far_segments)
    key_all = jnp.concatenate(key_list, axis=0)
    value_all = jnp.concatenate(value_list, axis=0)
    segment_all = jnp.concatenate(segment_list, axis=0)
    my_start = lax.axis_index("ctx") * tok_rows
    key_index = my_start - reach * tok_rows + jnp.arange((reach + 1) * tok_rows, dtype=jnp.int32)
    query_index = my_start + jnp.arange(tok_rows, dtype=jnp.int32)
    gap = query_index[:, None] - key_index[None, :]
    allowed = (
        (segment_ids[:, None] == segment_all[None, :])
        & (gap >= 0)
        & (gap < VISIBLE_SPAN)
        & (key_index[None, :] >= 0)
    )
    head_group = q_heads // kv_heads
    grouped = query_heads_all.reshape(tok_rows, kv_heads, head_group, HEAD_SIZE)
    scores = block_scores(grouped, key_all)
    scores = jnp.where(allowed[None, None], scores, MASKED)
    expo = jnp.exp(scores - jnp.max(scores, axis=-1, keepdims=True))
    weights = (expo / jnp.sum(expo, axis=-1, keepdims=True)).astype(jnp.bfloat16)
    mixed = block_mix(weights, value_all)
    attended = mixed.reshape(tok_rows, q_cols).astype(jnp.bfloat16)
    share = project_out(attended, out_full)
    squares = lax.psum(jnp.sum(share * share, axis=-1), "tp")
    branch = share * lax.rsqrt(squares[:, None] / MODEL_WIDTH + EPS) * post_gain
    return (inputs.astype(jnp.float32) + branch).astype(jnp.bfloat16)


def fits_planes(sizes):
    return sizes["tp"] == 2 and sizes["ctx"] == 16


def solution(mesh):
    sizes = mesh.shape
    return jax.shard_map(
        by_planes if fits_planes(sizes) else by_devices,
        mesh=mesh,
        in_specs=(
            P("ctx", "tp"),
            P(),
            P("ctx", "tp"),
            P("ctx", "tp"),
            P("ctx", "tp"),
            P(),
            P(),
            P("tp", "ctx"),
            P("tp"),
            P("ctx"),
            P("ctx"),
        ),
        out_specs=P("ctx", "tp"),
        check_vma=False,
    )
```

```python
import functools

import jax
import jax.numpy as jnp
from jax import lax
from jax.experimental import pallas as pl
from jax.experimental.pallas import tpu as pltpu
from jax.sharding import PartitionSpec as P

MODEL_WIDTH = 5376
QUERY_HEADS = 32
HEAD_SIZE = 128
VISIBLE_SPAN = 1024


EPS = 1e-06
ROPE_BASE = 10000.0
MASKED = -1e30

INNER = 4
QUERY_BLOCK = 256
TOKEN_BLOCK = 512
VMEM = 48 * 2**20


def rms_scale(values, gain):
    return values * lax.rsqrt(jnp.mean(values * values, axis=-1, keepdims=True) + EPS) * gain


def angles_of(position, half_dim):
    frequency = ROPE_BASE ** (-jnp.arange(half_dim, dtype=jnp.float32) / half_dim)
    angles = position.astype(jnp.float32)[:, None] * frequency[None, :]
    return jnp.cos(angles)[:, None, :], jnp.sin(angles)[:, None, :]


def rotate(values, cosine, sine):
    half_dim = values.shape[-1] // 2
    first = values[..., :half_dim]
    second = values[..., half_dim:]
    return jnp.concatenate(
        [first * cosine - second * sine, second * cosine + first * sine], axis=-1
    )


def prepare_heads(projected, gain, turn, factor):
    shaped = projected.reshape(projected.shape[0], -1, HEAD_SIZE)
    turned = rotate(rms_scale(shaped, gain), *turn) * factor
    return turned.astype(jnp.bfloat16).reshape(projected.shape)


def swap(x, mask):
    return lax.ppermute(x, "i", [(c, c ^ mask) for c in range(INNER)])


def swap_tp(x):
    return lax.ppermute(x, "tp", [(0, 1), (1, 0)])


def ring_step(x):
    size = lax.axis_size("z")
    return lax.ppermute(x, "z", [(c, (c + 1) % size) for c in range(size)])


def after(x, *others):
    return lax.optimization_barrier((x, *others))[0]


def in_order(first, mine, other):
    return jnp.where(first, jnp.stack([mine, other]), jnp.stack([other, mine]))


def norm_kernel(x_ref, gain_ref, o_ref):
    sides = [x_ref[0, side].astype(jnp.float32) for side in range(2)]
    squares = sum(jnp.sum(x * x, axis=-1, keepdims=True) for x in sides)
    scale = lax.rsqrt(squares / MODEL_WIDTH + EPS)
    per_side = o_ref.shape[0] // 2
    cols = o_ref.shape[2]
    for side, x in enumerate(sides):
        normed = (x * scale * gain_ref[side]).astype(jnp.bfloat16)
        for part in range(per_side):
            o_ref[side * per_side + part] = normed[:, part * cols : (part + 1) * cols]


def norm_by_blocks(gathered, in_gain, blocks):
    inner, sides, rows, cols = gathered.shape
    width = sides * cols // blocks
    step = 256
    per_place = rows // step
    return pl.pallas_call(
        norm_kernel,
        grid=(inner, per_place),
        in_specs=[
            pl.BlockSpec((1, sides, step, cols), lambda i, r: (i, 0, r, 0)),
            pl.BlockSpec((sides, 1, cols), lambda i, r: (0, 0, 0)),
        ],
        out_specs=pl.BlockSpec((blocks, step, width), lambda i, r: (0, i * per_place + r, 0)),
        out_shape=jax.ShapeDtypeStruct((blocks, inner * rows, width), jnp.bfloat16),
        compiler_params=pltpu.CompilerParams(vmem_limit_bytes=VMEM),
        cost_estimate=pl.CostEstimate(
            flops=5 * gathered.size, bytes_accessed=4 * gathered.size, transcendentals=0
        ),
    )(gathered, in_gain.reshape(sides, 1, cols))


def project_kernel(factor, source_ref, x_ref, *refs):
    blocks = x_ref.shape[0]
    weights, rest, o_ref = refs[:blocks], refs[blocks:-1], refs[-1]
    total = None
    for d in range(blocks):
        term = jnp.dot(x_ref[source_ref[d]], weights[d][...], preferred_element_type=jnp.float32)
        total = term if total is None else total + term
    if not rest:
        o_ref[...] = total.astype(jnp.bfloat16)
        return
    gain_ref, cos_ref, sin_ref = rest
    for head in range(total.shape[1] // HEAD_SIZE):
        span = slice(head * HEAD_SIZE, (head + 1) * HEAD_SIZE)
        values = total[:, span]
        values = rms_scale(values, gain_ref[...])
        turned = pltpu.roll(values, HEAD_SIZE // 2, 1)
        values = values * cos_ref[...] + turned * sin_ref[...]
        o_ref[:, span] = (values * factor).astype(jnp.bfloat16)


def project(normed, source, weights, gain=None, turn=None, factor=1.0):
    blocks, tokens, width = normed.shape
    cols = weights[0].shape[1]
    extra, extra_specs = [], []
    if gain is not None:
        extra = [gain.reshape(1, HEAD_SIZE), *turn]
        extra_specs = [pl.BlockSpec((1, HEAD_SIZE), lambda b: (0, 0))] + [
            pl.BlockSpec((TOKEN_BLOCK, HEAD_SIZE), lambda b: (b, 0))
        ] * 2
    return pl.pallas_call(
        functools.partial(project_kernel, factor),
        grid=(tokens // TOKEN_BLOCK,),
        in_specs=[
            pl.BlockSpec(memory_space=pltpu.SMEM),
            pl.BlockSpec((blocks, TOKEN_BLOCK, width), lambda b: (0, b, 0)),
        ]
        + [pl.BlockSpec((width, cols), lambda b: (0, 0))] * blocks
        + extra_specs,
        out_specs=pl.BlockSpec((TOKEN_BLOCK, cols), lambda b: (b, 0)),
        out_shape=jax.ShapeDtypeStruct((tokens, cols), jnp.bfloat16),
        compiler_params=pltpu.CompilerParams(vmem_limit_bytes=VMEM),
        cost_estimate=pl.CostEstimate(
            flops=2 * normed.size * cols,
            bytes_accessed=2 * (normed.size + blocks * width * cols + tokens * cols),
            transcendentals=0,
        ),
    )(source, normed, *weights, *extra)


def attend_kernel(pos_ref, q_ref, k_ref, v_ref, o_ref):
    start = pl.multiple_of(pl.program_id(0) * QUERY_BLOCK, QUERY_BLOCK)
    window = VISIBLE_SPAN + QUERY_BLOCK
    keys = k_ref[pl.ds(start, window), :]
    values = v_ref[pl.ds(start, window), :]
    shape = (QUERY_BLOCK, window)
    last = lax.broadcasted_iota(jnp.int32, shape, 0) + VISIBLE_SPAN
    column = lax.broadcasted_iota(jnp.int32, shape, 1)
    first = last - jnp.minimum(pos_ref[...], VISIBLE_SPAN - 1)
    allowed = (column <= last) & (column >= first)
    for head in range(q_ref.shape[1] // HEAD_SIZE):
        span = slice(head * HEAD_SIZE, (head + 1) * HEAD_SIZE)
        scores = lax.dot_general(
            q_ref[:, span], keys, (((1,), (1,)), ((), ())), preferred_element_type=jnp.float32
        )
        scores = jnp.where(allowed, scores, MASKED)
        expo = jnp.exp(scores - jnp.max(scores, axis=-1, keepdims=True))
        weights = (expo / jnp.sum(expo, axis=-1, keepdims=True)).astype(jnp.bfloat16)
        mixed = jnp.dot(weights, values, preferred_element_type=jnp.float32)
        o_ref[:, span] = mixed.astype(jnp.bfloat16)


def attend(position, queries, keys, values):
    tokens, cols = queries.shape
    window = VISIBLE_SPAN + QUERY_BLOCK
    heads = cols // HEAD_SIZE
    return pl.pallas_call(
        attend_kernel,
        grid=(tokens // QUERY_BLOCK,),
        in_specs=[
            pl.BlockSpec((QUERY_BLOCK, 1), lambda b: (b, 0)),
            pl.BlockSpec((QUERY_BLOCK, cols), lambda b: (b, 0)),
            pl.BlockSpec(keys.shape, lambda b: (0, 0)),
            pl.BlockSpec(values.shape, lambda b: (0, 0)),
        ],
        out_specs=pl.BlockSpec((QUERY_BLOCK, cols), lambda b: (b, 0)),
        out_shape=jax.ShapeDtypeStruct((tokens, cols), jnp.bfloat16),
        compiler_params=pltpu.CompilerParams(vmem_limit_bytes=VMEM),
        cost_estimate=pl.CostEstimate(
            flops=4 * tokens * window * cols,
            bytes_accessed=4 * tokens * cols + 4 * keys.shape[0] * HEAD_SIZE,
            transcendentals=heads * tokens * window,
        ),
    )(position, queries, keys, values)


def group_kernel(inner, pieces, place_ref, *refs):
    lefts, weight_ref, o_ref = refs[: inner * pieces], refs[-2], refs[-1]
    place = place_ref[0]
    depth = lefts[0].shape[1]
    total = None
    for m in range(inner):
        for piece in range(pieces):
            row = pl.multiple_of(((place ^ m) * pieces + piece) * depth, depth)
            term = lax.dot_general(
                weight_ref[:, pl.ds(row, depth)],
                lefts[m * pieces + piece][...],
                (((1,), (1,)), ((), ())),
                preferred_element_type=jnp.float32,
            )
            total = term if total is None else total + term
    o_ref[...] = total.astype(jnp.bfloat16)


def group_product(place, attended, weight):
    lefts = [piece for pieces in attended for piece in pieces]
    tokens, depth = lefts[0].shape
    cols, rows = weight.shape
    return pl.pallas_call(
        functools.partial(group_kernel, len(attended), len(attended[0])),
        grid=(tokens // TOKEN_BLOCK,),
        in_specs=[pl.BlockSpec(memory_space=pltpu.SMEM)]
        + [pl.BlockSpec((TOKEN_BLOCK, depth), lambda b: (b, 0)) for _ in lefts]
        + [pl.BlockSpec((cols, rows), lambda b: (0, 0))],
        out_specs=pl.BlockSpec((cols, TOKEN_BLOCK), lambda b: (0, b)),
        out_shape=jax.ShapeDtypeStruct((cols, tokens), jnp.bfloat16),
        compiler_params=pltpu.CompilerParams(vmem_limit_bytes=VMEM),
        cost_estimate=pl.CostEstimate(
            flops=2 * tokens * rows * cols,
            bytes_accessed=2 * (tokens * rows + rows * cols + tokens * cols),
            transcendentals=0,
        ),
    )(jnp.reshape(place, (1,)), *lefts, weight)


def shuffle_start(weights, place):
    def cut(which):
        parts = []
        for core in range(2):
            cols = [w.shape[1] // INNER for w in weights]
            spans = [
                lax.dynamic_slice_in_dim(w, (which * 2 + core) * n, n, axis=1)
                for w, n in zip(weights, cols)
            ]
            parts.append(jnp.concatenate(spans, axis=1) if len(spans) > 1 else spans[0])
        return jnp.stack(parts)

    side = place // 2
    return cut(side), swap(cut(1 - side), 2)


def shuffle_end(mine, theirs, place):
    core = place % 2
    rows = in_order(place // 2 == 0, mine, theirs)
    keep = lax.dynamic_index_in_dim(rows, core, 1, keepdims=False)
    give = lax.dynamic_index_in_dim(rows, 1 - core, 1, keepdims=False)
    whole = in_order(core == 0, keep, swap(give, 1))
    return whole.transpose(1, 0, 2, 3).reshape(-1, whole.shape[-1])


def by_planes(
    inputs,
    in_gain,
    q_weight,
    key_matrix,
    value_matrix,
    q_gain,
    key_norm_gain,
    out_weight,
    post_gain,
    segment_ids,
    positions,
):
    tok_rows = inputs.shape[0]
    planes = lax.axis_size("z")
    place, plane, side = lax.axis_index("i"), lax.axis_index("z"), lax.axis_index("tp")
    plane_tokens = INNER * tok_rows
    source = ((plane - jnp.arange(planes)) % planes).astype(jnp.int32)

    gathered = lax.all_gather(inputs, ("i", "tp"), axis=0, tiled=False)
    gathered = gathered.reshape(INNER, 2, *inputs.shape)

    kv_on_way = shuffle_start([key_matrix, value_matrix], place)
    out_rows = out_weight.T
    hops = {"o": [out_rows]}
    previous = []

    def hop(name, *others):
        block = hops[name][-1]
        hops[name].append(ring_step(after(block, *others) if others else block))
        previous.append(hops[name][-1])

    hop("o")
    pos_x = in_order(place // 2 == 0, positions, swap(positions, 2))
    q_on_way = shuffle_start([after(q_weight, kv_on_way[0])], place)
    kv = shuffle_end(*kv_on_way, place)
    kv_half = kv.shape[1] // 2
    hops["k"], hops["v"] = [kv[:, :kv_half]], [kv[:, kv_half:]]
    pos = in_order(place % 2 == 0, pos_x, swap(pos_x, 1)).transpose(1, 0, 2).reshape(-1)
    hop("k")
    hop("v")
    q = shuffle_end(*q_on_way, place)
    q_half = q.shape[1] // 2
    hops["qa"], hops["qb"] = [q[:, :q_half]], [q[:, q_half:]]
    order = ["k", "v"] * (planes - 2) + ["qa", "qb"] * (planes - 1) + ["o"] * (planes - 2)
    for name in order:
        hop(name, previous[-2])

    half = HEAD_SIZE // 2
    frequency = ROPE_BASE ** (-jnp.arange(half, dtype=jnp.float32) / half)
    angles = pos.astype(jnp.float32)[:, None] * frequency[None, :]
    cosine, sine = jnp.cos(angles), jnp.sin(angles)
    turn = (
        jnp.concatenate([cosine, cosine], axis=1),
        jnp.concatenate([-sine, sine], axis=1),
    )

    normed = norm_by_blocks(gathered, in_gain, planes)
    keys = project(normed, source, hops["k"], key_norm_gain, turn)
    values = project(normed, source, hops["v"])
    up = [(c, c + 1) for c in range(planes - 1)]
    own_kv = jnp.concatenate([keys, values], axis=1)
    halo = lax.ppermute(own_kv[plane_tokens - VISIBLE_SPAN :], "z", up)
    all_kv = jnp.concatenate([halo, own_kv], axis=0)

    factor = (MODEL_WIDTH // QUERY_HEADS) ** (-0.5)
    attended = [[] for _ in range(INNER)]
    for index, name in enumerate(("qa", "qb")):
        queries = project(normed, source, hops[name], q_gain, turn, factor)
        spans = [
            slice(n * HEAD_SIZE, (n + 1) * HEAD_SIZE) for n in (index, index + kv_half // HEAD_SIZE)
        ]
        own = attend(pos[:, None], queries, all_kv[:, spans[0]], all_kv[:, spans[1]])
        far = swap(own, 2)
        for mask, piece in zip(range(INNER), (own, swap(own, 1), far, swap(far, 1))):
            attended[mask].append(piece)

    axes = ("z", "i", "tp")
    cols = out_rows.shape[0]
    per_side = planes // 2
    slots = jnp.zeros((planes, INNER, cols, tok_rows), jnp.bfloat16)
    for d in range(planes):
        term = group_product(place, attended, hops["o"][d])
        across, inside = [], []
        for c in range(planes * INNER):
            home = ((c // INNER - d) % planes) // per_side
            across.append((2 * c + 1 - home, 2 * c + home))
            inside.append(2 * c + home)
        other = lax.ppermute(term, axes, across)
        total = (term.astype(jnp.float32) + other.astype(jnp.float32)).astype(jnp.bfloat16)
        for mask in range(INNER):
            block = lax.dynamic_slice_in_dim(total, (place ^ mask) * tok_rows, tok_rows, axis=1)
            if mask:
                block = lax.ppermute(block, axes, [(n, n ^ (2 * mask)) for n in inside])
            slots = lax.dynamic_update_slice(
                slots, block[None, None], (source[d], place ^ mask, 0, 0)
            )
    mine = lax.dynamic_slice_in_dim(slots, side * per_side, per_side, axis=0)
    share = mine.reshape(-1, tok_rows).astype(jnp.float32)
    own_squares = jnp.sum(share * share, axis=0)
    squares = own_squares + swap_tp(own_squares)
    branch = share * lax.rsqrt(squares / MODEL_WIDTH + EPS)[None, :] * post_gain[:, None]
    return (inputs.astype(jnp.float32) + branch.T).astype(jnp.bfloat16)


def from_behind(x, axis, by):
    size = lax.axis_size(axis)
    pairs = [(i, i + by) for i in range(size) if 0 <= i + by < size]
    return lax.ppermute(x, axis, pairs)


def block_scores(grouped, keys_block):
    return jnp.einsum("qhgd,khd->hgqk", grouped, keys_block, preferred_element_type=jnp.float32)


def block_mix(weights_block, values_block):
    return jnp.einsum(
        "hgqk,khd->qhgd", weights_block, values_block, preferred_element_type=jnp.float32
    )


def gather_features(inputs):
    if lax.axis_size("tp") != 2:
        return lax.all_gather(inputs, "tp", axis=1, tiled=True)
    other = lax.ppermute(inputs, "tp", [(0, 1), (1, 0)])
    first = lax.axis_index("tp") == 0
    return jnp.concatenate(
        [jnp.where(first, inputs, other), jnp.where(first, other, inputs)], axis=1
    )


def project_out(attended, out_full):
    if lax.axis_size("tp") != 2:
        partial_terms = jnp.dot(attended, out_full, preferred_element_type=jnp.float32)
        return lax.psum_scatter(
            partial_terms.astype(jnp.bfloat16), "tp", scatter_dimension=1, tiled=True
        ).astype(jnp.float32)
    here = lax.axis_index("tp")
    cols = out_full.shape[1] // 2

    def half(which):
        weight = lax.dynamic_slice_in_dim(out_full, which * cols, cols, axis=1)
        return jnp.dot(attended, weight, preferred_element_type=jnp.float32).astype(jnp.bfloat16)

    theirs = half(1 - here)
    arrived = lax.ppermute(theirs, "tp", [(0, 1), (1, 0)])
    return half(here).astype(jnp.float32) + arrived.astype(jnp.float32)


def by_devices(
    inputs,
    in_gain,
    q_weight,
    key_matrix,
    value_matrix,
    q_gain,
    key_norm_gain,
    out_weight,
    post_gain,
    segment_ids,
    positions,
):
    tok_rows = inputs.shape[0]
    q_cols = q_weight.shape[1]
    kv_cols = key_matrix.shape[1]
    stacked = jnp.concatenate([key_matrix, value_matrix, q_weight], axis=1)
    weights_full = lax.all_gather(stacked, "ctx", axis=0, tiled=True)
    out_full = lax.all_gather(out_weight, "ctx", axis=1, tiled=True)
    gathered = gather_features(inputs)
    normalized = rms_scale(gathered.astype(jnp.float32), in_gain).astype(jnp.bfloat16)
    raw = jnp.dot(normalized, weights_full, preferred_element_type=jnp.float32)
    k_raw = raw[:, :kv_cols]
    v_raw = raw[:, kv_cols : 2 * kv_cols]
    q_raw = raw[:, 2 * kv_cols :]
    q_heads = q_cols // HEAD_SIZE
    kv_heads = kv_cols // HEAD_SIZE
    turn = angles_of(positions, HEAD_SIZE // 2)
    query_heads_all = prepare_heads(
        q_raw, q_gain, turn, (MODEL_WIDTH // QUERY_HEADS) ** (-0.5)
    )
    keys_own = prepare_heads(k_raw, key_norm_gain, turn, 1.0)
    keys_own = keys_own.reshape(tok_rows, kv_heads, HEAD_SIZE)
    values_own = v_raw.reshape(tok_rows, kv_heads, HEAD_SIZE).astype(jnp.bfloat16)
    reach = (VISIBLE_SPAN - 1) // tok_rows + 1
    key_list = [keys_own]
    value_list = [values_own]
    segment_list = [segment_ids]
    for distance in range(1, reach + 1):
        far_keys, far_values, far_segments = from_behind(
            (keys_own, values_own, segment_ids), "ctx", distance
        )
        key_list.insert(0, far_keys)
        value_list.insert(0, far_values)
        segment_list.insert(0, far_segments)
    key_all = jnp.concatenate(key_list, axis=0)
    value_all = jnp.concatenate(value_list, axis=0)
    segment_all = jnp.concatenate(segment_list, axis=0)
    my_start = lax.axis_index("ctx") * tok_rows
    key_index = my_start - reach * tok_rows + jnp.arange((reach + 1) * tok_rows, dtype=jnp.int32)
    query_index = my_start + jnp.arange(tok_rows, dtype=jnp.int32)
    gap = query_index[:, None] - key_index[None, :]
    allowed = (
        (segment_ids[:, None] == segment_all[None, :])
        & (gap >= 0)
        & (gap < VISIBLE_SPAN)
        & (key_index[None, :] >= 0)
    )
    head_group = q_heads // kv_heads
    grouped = query_heads_all.reshape(tok_rows, kv_heads, head_group, HEAD_SIZE)
    scores = block_scores(grouped, key_all)
    scores = jnp.where(allowed[None, None], scores, MASKED)
    expo = jnp.exp(scores - jnp.max(scores, axis=-1, keepdims=True))
    weights = (expo / jnp.sum(expo, axis=-1, keepdims=True)).astype(jnp.bfloat16)
    mixed = block_mix(weights, value_all)
    attended = mixed.reshape(tok_rows, q_cols).astype(jnp.bfloat16)
    share = project_out(attended, out_full)
    squares = lax.psum(jnp.sum(share * share, axis=-1), "tp")
    branch = share * lax.rsqrt(squares[:, None] / MODEL_WIDTH + EPS) * post_gain
    return (inputs.astype(jnp.float32) + branch).astype(jnp.bfloat16)


def solution(mesh):
    ctx, tp = mesh.shape["ctx"], mesh.shape["tp"]
    whole_planes = tp == 2 and ctx % (2 * INNER) == 0
    if whole_planes:
        devices = mesh.devices.reshape(ctx // INNER, INNER, tp)
        mesh = jax.sharding.Mesh(devices, ("z", "i", "tp"))
    tokens = ("z", "i") if whole_planes else "ctx"
    return jax.shard_map(
        by_planes if whole_planes else by_devices,
        mesh=mesh,
        in_specs=(
            P(tokens, "tp"),
            P(),
            P(tokens, "tp"),
            P(tokens, "tp"),
            P(tokens, "tp"),
            P(),
            P(),
            P("tp", tokens),
            P("tp"),
            P(tokens),
            P(tokens),
        ),
        out_specs=P(tokens, "tp"),
        check_vma=False,
    )
```

```python
import functools

import jax
import jax.numpy as jnp
from jax import lax
from jax.experimental import pallas as pl
from jax.experimental.pallas import tpu as pltpu
from jax.sharding import PartitionSpec as P

MODEL_WIDTH = 5376
QUERY_HEADS = 32
HEAD_SIZE = 128
VISIBLE_SPAN = 1024


EPS = 1e-06
ROPE_BASE = 10000.0
MASKED = -1e30

INNER = 4
QUERY_BLOCK = 256
TOKEN_BLOCK = 512
VMEM = 48 * 2**20


def rms_scale(values, gain):
    return values * lax.rsqrt(jnp.mean(values * values, axis=-1, keepdims=True) + EPS) * gain


def angles_of(position, half_dim):
    frequency = ROPE_BASE ** (-jnp.arange(half_dim, dtype=jnp.float32) / half_dim)
    angles = position.astype(jnp.float32)[:, None] * frequency[None, :]
    return jnp.cos(angles)[:, None, :], jnp.sin(angles)[:, None, :]


def rotate(values, cosine, sine):
    half_dim = values.shape[-1] // 2
    first = values[..., :half_dim]
    second = values[..., half_dim:]
    return jnp.concatenate(
        [first * cosine - second * sine, second * cosine + first * sine], axis=-1
    )


def prepare_heads(projected, gain, turn, factor):
    shaped = projected.reshape(projected.shape[0], -1, HEAD_SIZE)
    turned = rotate(rms_scale(shaped, gain), *turn) * factor
    return turned.astype(jnp.bfloat16).reshape(projected.shape)


def swap(x, mask):
    return lax.ppermute(x, "i", [(c, c ^ mask) for c in range(INNER)])


def swap_tp(x):
    return lax.ppermute(x, "tp", [(0, 1), (1, 0)])


def ring_step(x):
    size = lax.axis_size("z")
    return lax.ppermute(x, "z", [(c, (c + 1) % size) for c in range(size)])


def after(x, *others):
    return lax.optimization_barrier((x, *others))[0]


def in_order(first, mine, other):
    return jnp.where(first, jnp.stack([mine, other]), jnp.stack([other, mine]))


def norm_kernel(x_ref, gain_ref, o_ref):
    sides = [x_ref[0, side].astype(jnp.float32) for side in range(2)]
    squares = sum(jnp.sum(x * x, axis=-1, keepdims=True) for x in sides)
    scale = lax.rsqrt(squares / MODEL_WIDTH + EPS)
    per_side = o_ref.shape[0] // 2
    cols = o_ref.shape[2]
    for side, x in enumerate(sides):
        normed = (x * scale * gain_ref[side]).astype(jnp.bfloat16)
        for part in range(per_side):
            o_ref[side * per_side + part] = normed[:, part * cols : (part + 1) * cols]


def norm_by_blocks(gathered, in_gain, blocks):
    inner, sides, rows, cols = gathered.shape
    width = sides * cols // blocks
    step = 256
    per_place = rows // step
    return pl.pallas_call(
        norm_kernel,
        grid=(inner, per_place),
        in_specs=[
            pl.BlockSpec((1, sides, step, cols), lambda i, r: (i, 0, r, 0)),
            pl.BlockSpec((sides, 1, cols), lambda i, r: (0, 0, 0)),
        ],
        out_specs=pl.BlockSpec((blocks, step, width), lambda i, r: (0, i * per_place + r, 0)),
        out_shape=jax.ShapeDtypeStruct((blocks, inner * rows, width), jnp.bfloat16),
        compiler_params=pltpu.CompilerParams(vmem_limit_bytes=VMEM),
        cost_estimate=pl.CostEstimate(
            flops=5 * gathered.size, bytes_accessed=4 * gathered.size, transcendentals=0
        ),
    )(gathered, in_gain.reshape(sides, 1, cols))


def project_kernel(factor, source_ref, x_ref, *refs):
    blocks = x_ref.shape[0]
    weights, rest, o_ref = refs[:blocks], refs[blocks:-1], refs[-1]
    total = None
    for d in range(blocks):
        term = jnp.dot(x_ref[source_ref[d]], weights[d][...], preferred_element_type=jnp.float32)
        total = term if total is None else total + term
    if not rest:
        o_ref[...] = total.astype(jnp.bfloat16)
        return
    gain_ref, cos_ref, sin_ref = rest
    for head in range(total.shape[1] // HEAD_SIZE):
        span = slice(head * HEAD_SIZE, (head + 1) * HEAD_SIZE)
        values = total[:, span]
        values = rms_scale(values, gain_ref[...])
        turned = pltpu.roll(values, HEAD_SIZE // 2, 1)
        values = values * cos_ref[...] + turned * sin_ref[...]
        o_ref[:, span] = (values * factor).astype(jnp.bfloat16)


def project(normed, source, weights, gain=None, turn=None, factor=1.0):
    blocks, tokens, width = normed.shape
    cols = weights[0].shape[1]
    extra, extra_specs = [], []
    if gain is not None:
        extra = [gain.reshape(1, HEAD_SIZE), *turn]
        extra_specs = [pl.BlockSpec((1, HEAD_SIZE), lambda b: (0, 0))] + [
            pl.BlockSpec((TOKEN_BLOCK, HEAD_SIZE), lambda b: (b, 0))
        ] * 2
    return pl.pallas_call(
        functools.partial(project_kernel, factor),
        grid=(tokens // TOKEN_BLOCK,),
        in_specs=[
            pl.BlockSpec(memory_space=pltpu.SMEM),
            pl.BlockSpec((blocks, TOKEN_BLOCK, width), lambda b: (0, b, 0)),
        ]
        + [pl.BlockSpec((width, cols), lambda b: (0, 0))] * blocks
        + extra_specs,
        out_specs=pl.BlockSpec((TOKEN_BLOCK, cols), lambda b: (b, 0)),
        out_shape=jax.ShapeDtypeStruct((tokens, cols), jnp.bfloat16),
        compiler_params=pltpu.CompilerParams(vmem_limit_bytes=VMEM),
        cost_estimate=pl.CostEstimate(
            flops=2 * normed.size * cols,
            bytes_accessed=2 * (normed.size + blocks * width * cols + tokens * cols),
            transcendentals=0,
        ),
    )(source, normed, *weights, *extra)


def attend_kernel(part, pos_ref, *refs):
    queries, (kv_ref, o_ref) = refs[:-2], refs[-2:]
    start = pl.multiple_of((pl.program_id(0) * 2 + part) * QUERY_BLOCK, QUERY_BLOCK)
    window = VISIBLE_SPAN + QUERY_BLOCK
    shape = (QUERY_BLOCK, window)
    last = lax.broadcasted_iota(jnp.int32, shape, 0) + VISIBLE_SPAN
    column = lax.broadcasted_iota(jnp.int32, shape, 1)
    first = last - jnp.minimum(pos_ref[...], VISIBLE_SPAN - 1)
    allowed = (column <= last) & (column >= first)
    kv_heads = len(queries)
    for kv_head, q_ref in enumerate(queries):
        keys = kv_ref[pl.ds(start, window), pl.ds(kv_head * HEAD_SIZE, HEAD_SIZE)]
        values = kv_ref[pl.ds(start, window), pl.ds((kv_heads + kv_head) * HEAD_SIZE, HEAD_SIZE)]
        group = q_ref.shape[1] // HEAD_SIZE
        for head in range(group):
            span = slice(head * HEAD_SIZE, (head + 1) * HEAD_SIZE)
            scores = lax.dot_general(
                q_ref[:, span], keys, (((1,), (1,)), ((), ())), preferred_element_type=jnp.float32
            )
            scores = jnp.where(allowed, scores, MASKED)
            expo = jnp.exp(scores - jnp.max(scores, axis=-1, keepdims=True))
            weights = (expo / jnp.sum(expo, axis=-1, keepdims=True)).astype(jnp.bfloat16)
            mixed = jnp.dot(weights, values, preferred_element_type=jnp.float32)
            place = (kv_head * group + head) * HEAD_SIZE
            o_ref[:, place : place + HEAD_SIZE] = mixed.astype(jnp.bfloat16)


def attend(part, position, queries, all_kv):
    tokens, cols = queries[0].shape
    window = VISIBLE_SPAN + QUERY_BLOCK
    width = cols * len(queries)
    half = tokens // 2
    return pl.pallas_call(
        functools.partial(attend_kernel, part),
        grid=(half // QUERY_BLOCK,),
        in_specs=[pl.BlockSpec((QUERY_BLOCK, 1), lambda b: (2 * b + part, 0))]
        + [pl.BlockSpec((QUERY_BLOCK, cols), lambda b: (2 * b + part, 0)) for _ in queries]
        + [pl.BlockSpec(all_kv.shape, lambda b: (0, 0))],
        out_specs=pl.BlockSpec((QUERY_BLOCK, width), lambda b: (b, 0)),
        out_shape=jax.ShapeDtypeStruct((half, width), jnp.bfloat16),
        compiler_params=pltpu.CompilerParams(vmem_limit_bytes=VMEM),
        cost_estimate=pl.CostEstimate(
            flops=4 * half * window * width,
            bytes_accessed=4 * half * width + 2 * all_kv.size,
            transcendentals=half * window * width // HEAD_SIZE,
        ),
    )(position, *queries, all_kv)


def group_kernel(inner, place_ref, source_ref, *refs):
    lefts, weights, o_ref = refs[:inner], refs[inner:-1], refs[-1]
    place = place_ref[0]
    depth = lefts[0].shape[1]
    for d, weight_ref in enumerate(weights):
        total = None
        for m in range(inner):
            row = pl.multiple_of((place ^ m) * depth, depth)
            term = lax.dot_general(
                weight_ref[:, pl.ds(row, depth)],
                lefts[m][...],
                (((1,), (1,)), ((), ())),
                preferred_element_type=jnp.float32,
            )
            total = term if total is None else total + term
        o_ref[source_ref[d]] = total.astype(jnp.bfloat16)


def group_product(place, source, attended, weights):
    tokens, depth = attended[0].shape
    cols, rows = weights[0].shape
    blocks = len(weights)
    return pl.pallas_call(
        functools.partial(group_kernel, len(attended)),
        grid=(tokens // TOKEN_BLOCK,),
        in_specs=[pl.BlockSpec(memory_space=pltpu.SMEM)] * 2
        + [pl.BlockSpec((TOKEN_BLOCK, depth), lambda b: (b, 0)) for _ in attended]
        + [pl.BlockSpec((cols, rows), lambda b: (0, 0)) for _ in weights],
        out_specs=pl.BlockSpec((blocks, cols, TOKEN_BLOCK), lambda b: (0, 0, b)),
        out_shape=jax.ShapeDtypeStruct((blocks, cols, tokens), jnp.bfloat16),
        compiler_params=pltpu.CompilerParams(vmem_limit_bytes=VMEM),
        cost_estimate=pl.CostEstimate(
            flops=2 * tokens * rows * cols * blocks,
            bytes_accessed=2 * (tokens * rows + (rows + tokens) * cols * blocks),
            transcendentals=0,
        ),
    )(jnp.reshape(place, (1,)), source, *attended, *weights)


def shuffle_start(weights, place):
    def cut(which):
        parts = []
        for core in range(2):
            cols = [w.shape[1] // INNER for w in weights]
            spans = [
                lax.dynamic_slice_in_dim(w, (which * 2 + core) * n, n, axis=1)
                for w, n in zip(weights, cols)
            ]
            parts.append(jnp.concatenate(spans, axis=1) if len(spans) > 1 else spans[0])
        return jnp.stack(parts)

    side = place // 2
    return cut(side), swap(cut(1 - side), 2)


def shuffle_end(mine, theirs, place):
    core = place % 2
    rows = in_order(place // 2 == 0, mine, theirs)
    keep = lax.dynamic_index_in_dim(rows, core, 1, keepdims=False)
    give = lax.dynamic_index_in_dim(rows, 1 - core, 1, keepdims=False)
    whole = in_order(core == 0, keep, swap(give, 1))
    return whole.transpose(1, 0, 2, 3).reshape(-1, whole.shape[-1])


def by_planes(
    inputs,
    in_gain,
    q_weight,
    key_matrix,
    value_matrix,
    q_gain,
    key_norm_gain,
    out_weight,
    post_gain,
    segment_ids,
    positions,
):
    tok_rows = inputs.shape[0]
    planes = lax.axis_size("z")
    place, plane, side = lax.axis_index("i"), lax.axis_index("z"), lax.axis_index("tp")
    plane_tokens = INNER * tok_rows
    source = ((plane - jnp.arange(planes)) % planes).astype(jnp.int32)

    gathered = lax.all_gather(inputs, ("i", "tp"), axis=0, tiled=False)
    gathered = gathered.reshape(INNER, 2, *inputs.shape)

    kv_on_way = shuffle_start([key_matrix, value_matrix], place)
    out_rows = out_weight.T
    hops = {"o": [out_rows]}
    previous = []

    def hop(name, *others):
        block = hops[name][-1]
        hops[name].append(ring_step(after(block, *others) if others else block))
        previous.append(hops[name][-1])

    hop("o")
    pos_x = in_order(place // 2 == 0, positions, swap(positions, 2))
    q_on_way = shuffle_start([after(q_weight, kv_on_way[0])], place)
    kv = shuffle_end(kv_on_way[0], after(kv_on_way[1], hops["o"][1]), place)
    kv_half = kv.shape[1] // 2
    hops["k"], hops["v"] = [kv[:, :kv_half]], [kv[:, kv_half:]]
    pos = in_order(place % 2 == 0, pos_x, swap(pos_x, 1)).transpose(1, 0, 2).reshape(-1)
    hop("k")
    hop("v")
    q = shuffle_end(q_on_way[0], after(q_on_way[1], hops["k"][1]), place)
    q_half = q.shape[1] // 2
    hops["qa"], hops["qb"] = [q[:, :q_half]], [q[:, q_half:]]
    for name in ["k", "v"] * (planes - 2):
        hop(name, previous[-2])
    hop("qa", previous[-2])
    hop("qb", previous[-2])

    half = HEAD_SIZE // 2
    frequency = ROPE_BASE ** (-jnp.arange(half, dtype=jnp.float32) / half)
    angles = pos.astype(jnp.float32)[:, None] * frequency[None, :]
    cosine, sine = jnp.cos(angles), jnp.sin(angles)
    turn = (
        jnp.concatenate([cosine, cosine], axis=1),
        jnp.concatenate([-sine, sine], axis=1),
    )

    normed = norm_by_blocks(after(gathered, hops["v"][-1], *turn), in_gain, planes)
    hop("qa", normed)
    hop("qb", normed)
    keys = project(after(normed, hops["qb"][-2]), source, hops["k"], key_norm_gain, turn)
    for _ in range(planes - 3):
        hop("qa", keys)
        hop("qb", keys)
    values = project(after(normed, hops["qa"][-2], keys), source, hops["v"])
    up = [(c, c + 1) for c in range(planes - 1)]
    own_kv = jnp.concatenate([keys, values], axis=1)
    halo = lax.ppermute(own_kv[plane_tokens - VISIBLE_SPAN :], "z", up)
    all_kv = jnp.concatenate([halo, own_kv], axis=0)
    for _ in range(planes - 2):
        hop("o", previous[-2])

    factor = (MODEL_WIDTH // QUERY_HEADS) ** (-0.5)
    queries = [
        project(after(normed, values), source, hops[name], q_gain, turn, factor)
        for name in ("qa", "qb")
    ]

    own = [attend(0, pos[:, None], queries, all_kv)]
    own.append(attend(1, after(pos, own[0], hops["o"][-2])[:, None], queries, all_kv))
    here = place // 2, place % 2
    per_side = planes // 2
    results = []
    for part in range(2):
        far = swap(own[part], 2)
        attended = [own[part], swap(own[part], 1), far, swap(far, 1)]
        if part == 0:
            attended[0] = after(own[0], own[1])
        terms = group_product(place, source, attended, hops["o"])
        keep = lax.dynamic_slice_in_dim(terms, side * per_side, per_side, axis=0)
        give = lax.dynamic_slice_in_dim(terms, (1 - side) * per_side, per_side, axis=0)
        sums = (keep.astype(jnp.float32) + swap_tp(give).astype(jnp.float32)).astype(jnp.bfloat16)
        for bit, mask in ((0, 2), (1, 1)):
            width = sums.shape[-1] // 2
            keep = lax.dynamic_slice_in_dim(sums, here[bit] * width, width, axis=-1)
            give = lax.dynamic_slice_in_dim(sums, (1 - here[bit]) * width, width, axis=-1)
            sums = in_order(here[bit] == 0, keep, swap(give, mask))
        share = sums.transpose(2, 1, 0, 3, 4).reshape(-1, sums.shape[-1]).astype(jnp.float32)
        own_squares = jnp.sum(share * share, axis=0)
        squares = own_squares + swap_tp(own_squares)
        branch = share * lax.rsqrt(squares / MODEL_WIDTH + EPS)[None, :] * post_gain[:, None]
        rows = inputs[part * QUERY_BLOCK : (part + 1) * QUERY_BLOCK].astype(jnp.float32)
        results.append((rows + branch.T).astype(jnp.bfloat16))
    return jnp.concatenate(results, axis=0)


def from_behind(x, axis, by):
    size = lax.axis_size(axis)
    pairs = [(i, i + by) for i in range(size) if 0 <= i + by < size]
    return lax.ppermute(x, axis, pairs)


def block_scores(grouped, keys_block):
    return jnp.einsum("qhgd,khd->hgqk", grouped, keys_block, preferred_element_type=jnp.float32)


def block_mix(weights_block, values_block):
    return jnp.einsum(
        "hgqk,khd->qhgd", weights_block, values_block, preferred_element_type=jnp.float32
    )


def gather_features(inputs):
    if lax.axis_size("tp") != 2:
        return lax.all_gather(inputs, "tp", axis=1, tiled=True)
    other = lax.ppermute(inputs, "tp", [(0, 1), (1, 0)])
    first = lax.axis_index("tp") == 0
    return jnp.concatenate(
        [jnp.where(first, inputs, other), jnp.where(first, other, inputs)], axis=1
    )


def project_out(attended, out_full):
    if lax.axis_size("tp") != 2:
        partial_terms = jnp.dot(attended, out_full, preferred_element_type=jnp.float32)
        return lax.psum_scatter(
            partial_terms.astype(jnp.bfloat16), "tp", scatter_dimension=1, tiled=True
        ).astype(jnp.float32)
    here = lax.axis_index("tp")
    cols = out_full.shape[1] // 2

    def half(which):
        weight = lax.dynamic_slice_in_dim(out_full, which * cols, cols, axis=1)
        return jnp.dot(attended, weight, preferred_element_type=jnp.float32).astype(jnp.bfloat16)

    theirs = half(1 - here)
    arrived = lax.ppermute(theirs, "tp", [(0, 1), (1, 0)])
    return half(here).astype(jnp.float32) + arrived.astype(jnp.float32)


def by_devices(
    inputs,
    in_gain,
    q_weight,
    key_matrix,
    value_matrix,
    q_gain,
    key_norm_gain,
    out_weight,
    post_gain,
    segment_ids,
    positions,
):
    tok_rows = inputs.shape[0]
    q_cols = q_weight.shape[1]
    kv_cols = key_matrix.shape[1]
    stacked = jnp.concatenate([key_matrix, value_matrix, q_weight], axis=1)
    weights_full = lax.all_gather(stacked, "ctx", axis=0, tiled=True)
    out_full = lax.all_gather(out_weight, "ctx", axis=1, tiled=True)
    gathered = gather_features(inputs)
    normalized = rms_scale(gathered.astype(jnp.float32), in_gain).astype(jnp.bfloat16)
    raw = jnp.dot(normalized, weights_full, preferred_element_type=jnp.float32)
    k_raw = raw[:, :kv_cols]
    v_raw = raw[:, kv_cols : 2 * kv_cols]
    q_raw = raw[:, 2 * kv_cols :]
    q_heads = q_cols // HEAD_SIZE
    kv_heads = kv_cols // HEAD_SIZE
    turn = angles_of(positions, HEAD_SIZE // 2)
    query_heads_all = prepare_heads(
        q_raw, q_gain, turn, (MODEL_WIDTH // QUERY_HEADS) ** (-0.5)
    )
    keys_own = prepare_heads(k_raw, key_norm_gain, turn, 1.0)
    keys_own = keys_own.reshape(tok_rows, kv_heads, HEAD_SIZE)
    values_own = v_raw.reshape(tok_rows, kv_heads, HEAD_SIZE).astype(jnp.bfloat16)
    reach = (VISIBLE_SPAN - 1) // tok_rows + 1
    key_list = [keys_own]
    value_list = [values_own]
    segment_list = [segment_ids]
    for distance in range(1, reach + 1):
        far_keys, far_values, far_segments = from_behind(
            (keys_own, values_own, segment_ids), "ctx", distance
        )
        key_list.insert(0, far_keys)
        value_list.insert(0, far_values)
        segment_list.insert(0, far_segments)
    key_all = jnp.concatenate(key_list, axis=0)
    value_all = jnp.concatenate(value_list, axis=0)
    segment_all = jnp.concatenate(segment_list, axis=0)
    my_start = lax.axis_index("ctx") * tok_rows
    key_index = my_start - reach * tok_rows + jnp.arange((reach + 1) * tok_rows, dtype=jnp.int32)
    query_index = my_start + jnp.arange(tok_rows, dtype=jnp.int32)
    gap = query_index[:, None] - key_index[None, :]
    allowed = (
        (segment_ids[:, None] == segment_all[None, :])
        & (gap >= 0)
        & (gap < VISIBLE_SPAN)
        & (key_index[None, :] >= 0)
    )
    head_group = q_heads // kv_heads
    grouped = query_heads_all.reshape(tok_rows, kv_heads, head_group, HEAD_SIZE)
    scores = block_scores(grouped, key_all)
    scores = jnp.where(allowed[None, None], scores, MASKED)
    expo = jnp.exp(scores - jnp.max(scores, axis=-1, keepdims=True))
    weights = (expo / jnp.sum(expo, axis=-1, keepdims=True)).astype(jnp.bfloat16)
    mixed = block_mix(weights, value_all)
    attended = mixed.reshape(tok_rows, q_cols).astype(jnp.bfloat16)
    share = project_out(attended, out_full)
    squares = lax.psum(jnp.sum(share * share, axis=-1), "tp")
    branch = share * lax.rsqrt(squares[:, None] / MODEL_WIDTH + EPS) * post_gain
    return (inputs.astype(jnp.float32) + branch).astype(jnp.bfloat16)


def solution(mesh):
    ctx, tp = mesh.shape["ctx"], mesh.shape["tp"]
    whole_planes = tp == 2 and ctx % (2 * INNER) == 0
    if whole_planes:
        devices = mesh.devices.reshape(ctx // INNER, INNER, tp)
        mesh = jax.sharding.Mesh(devices, ("z", "i", "tp"))
    tokens = ("z", "i") if whole_planes else "ctx"
    return jax.shard_map(
        by_planes if whole_planes else by_devices,
        mesh=mesh,
        in_specs=(
            P(tokens, "tp"),
            P(),
            P(tokens, "tp"),
            P(tokens, "tp"),
            P(tokens, "tp"),
            P(),
            P(),
            P("tp", tokens),
            P("tp"),
            P(tokens),
            P(tokens),
        ),
        out_specs=P(tokens, "tp"),
        check_vma=False,
    )
```

```python
import functools

import jax
import jax.numpy as jnp
from jax import lax
from jax.experimental import pallas as pl
from jax.experimental.pallas import tpu as pltpu
from jax.sharding import PartitionSpec as P

MODEL_WIDTH = 5376
QUERY_HEADS = 32
HEAD_SIZE = 128
VISIBLE_SPAN = 1024


EPS = 1e-06
ROPE_BASE = 10000.0
MASKED = -1e30

INNER = 4
QUERY_BLOCK = 256
TOKEN_BLOCK = 512
MIB = 2**20


def lasting(microseconds):
    return pl.CostEstimate(flops=int(microseconds * 1e9), bytes_accessed=0, transcendentals=0)


def rms_scale(values, gain):
    return values * lax.rsqrt(jnp.mean(values * values, axis=-1, keepdims=True) + EPS) * gain


def angles_of(position, half_dim):
    frequency = ROPE_BASE ** (-jnp.arange(half_dim, dtype=jnp.float32) / half_dim)
    angles = position.astype(jnp.float32)[:, None] * frequency[None, :]
    return jnp.cos(angles)[:, None, :], jnp.sin(angles)[:, None, :]


def rotate(values, cosine, sine):
    half_dim = values.shape[-1] // 2
    first = values[..., :half_dim]
    second = values[..., half_dim:]
    return jnp.concatenate(
        [first * cosine - second * sine, second * cosine + first * sine], axis=-1
    )


def prepare_heads(projected, gain, turn, factor):
    shaped = projected.reshape(projected.shape[0], -1, HEAD_SIZE)
    turned = rotate(rms_scale(shaped, gain), *turn) * factor
    return turned.astype(jnp.bfloat16).reshape(projected.shape)


def swap(x, mask):
    return lax.ppermute(x, "i", [(c, c ^ mask) for c in range(INNER)])


def swap_tp(x):
    return lax.ppermute(x, "tp", [(0, 1), (1, 0)])


def ring_step(x):
    size = lax.axis_size("z")
    return lax.ppermute(x, "z", [(c, (c + 1) % size) for c in range(size)])


def after(x, *others):
    return lax.optimization_barrier((x, *others))[0]


def in_order(first, mine, other):
    return jnp.where(first, jnp.stack([mine, other]), jnp.stack([other, mine]))


def project_kernel(factor, turned_cols, blocks, source_ref, x_ref, *refs):
    o_ref, whole_ref = refs[-2:]
    gain_ref, cos_ref, sin_ref = refs[-5:-2]
    weights = refs[:-5]

    @pl.when(pl.program_id(0) == 0)
    def _():
        for n, weight_ref in enumerate(weights):
            height, width = weight_ref.shape
            row = pl.multiple_of(source_ref[n % blocks] * height, 64)
            col = n // blocks * width
            whole_ref[pl.ds(row, height), col : col + width] = weight_ref[...]

    depth = x_ref.shape[-1]
    total = None
    for side in range(x_ref.shape[1]):
        term = jnp.dot(
            x_ref[0, side],
            whole_ref[side * depth : (side + 1) * depth, :],
            preferred_element_type=jnp.float32,
        )
        total = term if total is None else total + term
    for head in range(turned_cols // HEAD_SIZE):
        span = slice(head * HEAD_SIZE, (head + 1) * HEAD_SIZE)
        values = rms_scale(total[:, span], gain_ref[...])
        turned = pltpu.roll(values, HEAD_SIZE // 2, 1)
        values = values * cos_ref[...] + turned * sin_ref[...]
        o_ref[:, span] = (values * factor).astype(jnp.bfloat16)
    if turned_cols < total.shape[1]:
        o_ref[:, turned_cols:] = total[:, turned_cols:].astype(jnp.bfloat16)


def project(normed, source, groups, turned_groups, gain, turn, factor=1.0):
    inner, sides, rows, depth = normed.shape
    height, width = groups[0][0].shape
    cols = width * len(groups)
    weights = [block for group in groups for block in group]
    tokens = inner * rows
    return pl.pallas_call(
        functools.partial(project_kernel, factor, turned_groups * width, len(groups[0])),
        grid=(inner,),
        in_specs=[
            pl.BlockSpec(memory_space=pltpu.SMEM),
            pl.BlockSpec((1, sides, rows, depth), lambda b: (b, 0, 0, 0)),
        ]
        + [pl.BlockSpec((height, width), lambda b: (0, 0)) for _ in weights]
        + [pl.BlockSpec((1, HEAD_SIZE), lambda b: (0, 0))]
        + [pl.BlockSpec((rows, HEAD_SIZE), lambda b: (b, 0)) for _ in turn],
        out_specs=pl.BlockSpec((rows, cols), lambda b: (b, 0)),
        out_shape=jax.ShapeDtypeStruct((tokens, cols), jnp.bfloat16),
        scratch_shapes=[pltpu.VMEM((sides * depth, cols), jnp.bfloat16)],
        compiler_params=pltpu.CompilerParams(vmem_limit_bytes=36 * MIB),
        cost_estimate=lasting(width / 26),
    )(source, normed, *weights, gain.reshape(1, HEAD_SIZE), *turn)


def attend_kernel(part, pos_ref, *refs):
    queries, (kv_ref, o_ref) = refs[:-2], refs[-2:]
    start = pl.multiple_of((pl.program_id(0) * 2 + part) * QUERY_BLOCK, QUERY_BLOCK)
    window = VISIBLE_SPAN + QUERY_BLOCK
    shape = (QUERY_BLOCK, window)
    last = lax.broadcasted_iota(jnp.int32, shape, 0) + VISIBLE_SPAN
    column = lax.broadcasted_iota(jnp.int32, shape, 1)
    first = last - jnp.minimum(pos_ref[...], VISIBLE_SPAN - 1)
    allowed = (column <= last) & (column >= first)
    kv_heads = len(queries)
    for kv_head, q_ref in enumerate(queries):
        keys = kv_ref[pl.ds(start, window), pl.ds(kv_head * HEAD_SIZE, HEAD_SIZE)]
        values = kv_ref[pl.ds(start, window), pl.ds((kv_heads + kv_head) * HEAD_SIZE, HEAD_SIZE)]
        group = q_ref.shape[1] // HEAD_SIZE
        for head in range(group):
            span = slice(head * HEAD_SIZE, (head + 1) * HEAD_SIZE)
            scores = lax.dot_general(
                q_ref[:, span], keys, (((1,), (1,)), ((), ())), preferred_element_type=jnp.float32
            )
            scores = jnp.where(allowed, scores, MASKED)
            expo = jnp.exp(scores - jnp.max(scores, axis=-1, keepdims=True))
            weights = (expo / jnp.sum(expo, axis=-1, keepdims=True)).astype(jnp.bfloat16)
            mixed = jnp.dot(weights, values, preferred_element_type=jnp.float32)
            place = (kv_head * group + head) * HEAD_SIZE
            o_ref[:, place : place + HEAD_SIZE] = mixed.astype(jnp.bfloat16)


def attend(part, position, queries, all_kv):
    tokens, cols = queries[0].shape
    window = VISIBLE_SPAN + QUERY_BLOCK
    width = cols * len(queries)
    half = tokens // 2
    return pl.pallas_call(
        functools.partial(attend_kernel, part),
        grid=(half // QUERY_BLOCK,),
        in_specs=[pl.BlockSpec((QUERY_BLOCK, 1), lambda b: (2 * b + part, 0))]
        + [pl.BlockSpec((QUERY_BLOCK, cols), lambda b: (2 * b + part, 0)) for _ in queries]
        + [pl.BlockSpec(all_kv.shape, lambda b: (0, 0))],
        out_specs=pl.BlockSpec((QUERY_BLOCK, width), lambda b: (b, 0)),
        out_shape=jax.ShapeDtypeStruct((half, width), jnp.bfloat16),
        compiler_params=pltpu.CompilerParams(vmem_limit_bytes=20 * MIB),
        cost_estimate=lasting(14.5),
    )(position, *queries, all_kv)


def group_kernel(inner, place_ref, kept_ref, *refs):
    pairs = kept_ref.shape[0]
    lefts, weights, outs = refs[:inner], refs[inner : inner + 2 * pairs], refs[inner + 2 * pairs :]
    place = place_ref[0]
    depth = lefts[0].shape[1]
    for n, weight_ref in enumerate(weights):
        total = None
        for m in range(inner):
            row = pl.multiple_of((place ^ m) * depth, depth)
            term = lax.dot_general(
                weight_ref[:, pl.ds(row, depth)],
                lefts[m][...],
                (((1,), (1,)), ((), ())),
                preferred_element_type=jnp.float32,
            )
            total = term if total is None else total + term
        total = total.astype(jnp.bfloat16)
        kept = kept_ref[n // 2]
        for out, which in zip(outs[n // 2 * 2 : n // 2 * 2 + 2], (kept, 1 - kept)):

            @pl.when(which == n % 2)
            def _():
                out[...] = total


def group_product(place, kept, attended, weights):
    tokens, depth = attended[0].shape
    cols, rows = weights[0].shape
    shape = jax.ShapeDtypeStruct((cols, tokens), jnp.bfloat16)
    return pl.pallas_call(
        functools.partial(group_kernel, len(attended)),
        grid=(tokens // TOKEN_BLOCK,),
        in_specs=[pl.BlockSpec(memory_space=pltpu.SMEM)] * 2
        + [pl.BlockSpec((TOKEN_BLOCK, depth), lambda b: (b, 0)) for _ in attended]
        + [pl.BlockSpec((cols, rows), lambda b: (0, 0)) for _ in weights],
        out_specs=[pl.BlockSpec((cols, TOKEN_BLOCK), lambda b: (0, b))] * len(weights),
        out_shape=[shape] * len(weights),
        compiler_params=pltpu.CompilerParams(vmem_limit_bytes=24 * MIB),
        cost_estimate=lasting(2.9 * len(weights)),
    )(jnp.reshape(place, (1,)), jnp.stack(kept).astype(jnp.int32), *attended, *weights)


def squares_kernel(*refs):
    total = None
    for ref in refs[:-1]:
        values = ref[...].astype(jnp.float32)
        term = jnp.sum(values * values, axis=0, keepdims=True)
        total = term if total is None else total + term
    refs[-1][...] = total


def squares_of(blocks):
    return pl.pallas_call(
        squares_kernel,
        out_shape=jax.ShapeDtypeStruct((1, blocks[0].shape[1]), jnp.float32),
        compiler_params=pltpu.CompilerParams(vmem_limit_bytes=8 * MIB),
    )(*blocks)


def finish_kernel(count, slots_ref, own_ref, other_ref, gain_ref, input_ref, *refs):
    blocks, (o_ref, share_ref) = refs[:count], refs[-2:]
    height = blocks[0].shape[0]
    for n, block in enumerate(blocks):
        row = pl.multiple_of(slots_ref[n] * height, 16)
        share_ref[pl.ds(row, height), :] = block[...]
    scale = lax.rsqrt((own_ref[...] + other_ref[...]) / MODEL_WIDTH + EPS)
    for col in range(0, share_ref.shape[0], HEAD_SIZE):
        span = slice(col, col + HEAD_SIZE)
        branch = (share_ref[span, :].astype(jnp.float32) * scale).T * gain_ref[:, span]
        o_ref[:, span] = (input_ref[:, span].astype(jnp.float32) + branch).astype(jnp.bfloat16)


def finish(part, slots, own, other, gain, inputs, blocks, so_far):
    rows, cols = inputs.shape
    step = blocks[0].shape[1]
    whole = lambda x: pl.BlockSpec(x.shape, lambda b: (0, 0))
    extra = [] if so_far is None else [so_far]
    operands = [slots, own, other, gain.reshape(1, cols), inputs, *blocks, *extra]
    return pl.pallas_call(
        functools.partial(finish_kernel, len(blocks)),
        grid=(1,),
        in_specs=[pl.BlockSpec(memory_space=pltpu.SMEM), whole(own), whole(other), whole(operands[3])]
        + [pl.BlockSpec((step, cols), lambda b: (part, 0))]
        + [whole(block) for block in blocks]
        + [pl.BlockSpec(memory_space=pl.ANY) for _ in extra],
        out_specs=pl.BlockSpec((step, cols), lambda b: (part, 0)),
        out_shape=jax.ShapeDtypeStruct((rows, cols), jnp.bfloat16),
        scratch_shapes=[pltpu.VMEM((cols, step), jnp.bfloat16)],
        input_output_aliases={len(operands) - 1: 0} if extra else {},
        compiler_params=pltpu.CompilerParams(vmem_limit_bytes=16 * MIB),
    )(*operands)


def shuffle_start(weights, place):
    def cut(which):
        parts = []
        for core in range(2):
            cols = [w.shape[1] // INNER for w in weights]
            spans = [
                lax.dynamic_slice_in_dim(w, (which * 2 + core) * n, n, axis=1)
                for w, n in zip(weights, cols)
            ]
            parts.append(jnp.concatenate(spans, axis=1) if len(spans) > 1 else spans[0])
        return jnp.stack(parts)

    side = place // 2
    return cut(side), swap(cut(1 - side), 2)


def shuffle_end(mine, theirs, place):
    core = place % 2
    rows = in_order(place // 2 == 0, mine, theirs)
    keep = lax.dynamic_index_in_dim(rows, core, 1, keepdims=False)
    give = lax.dynamic_index_in_dim(rows, 1 - core, 1, keepdims=False)
    whole = in_order(core == 0, keep, swap(give, 1))
    return whole.transpose(1, 0, 2, 3).reshape(-1, whole.shape[-1])


def by_planes(
    inputs,
    in_gain,
    q_weight,
    key_matrix,
    value_matrix,
    q_gain,
    key_norm_gain,
    out_weight,
    post_gain,
    segment_ids,
    positions,
):
    tok_rows = inputs.shape[0]
    planes = lax.axis_size("z")
    place, plane, side = lax.axis_index("i"), lax.axis_index("z"), lax.axis_index("tp")
    plane_tokens = INNER * tok_rows
    source = ((plane - jnp.arange(planes)) % planes).astype(jnp.int32)

    kv_on_way = shuffle_start([key_matrix, value_matrix], place)
    out_rows = out_weight.T
    hops = {"o": [out_rows]}
    previous = []

    def hop(name, *others):
        block = hops[name][-1]
        hops[name].append(ring_step(after(block, *others) if others else block))
        previous.append(hops[name][-1])

    hop("o")
    values = inputs.astype(jnp.float32)
    squares = jnp.sum(values * values, axis=-1)
    scale = lax.rsqrt((squares + swap_tp(squares)) / MODEL_WIDTH + EPS)
    gain = lax.dynamic_slice_in_dim(in_gain, side * inputs.shape[1], inputs.shape[1])
    normed = (values * scale[:, None] * gain).astype(jnp.bfloat16)
    normed = lax.all_gather(normed, ("i", "tp"), axis=0, tiled=False)
    normed = normed.reshape(INNER, 2, *inputs.shape)

    pos_x = in_order(place // 2 == 0, positions, swap(positions, 2))
    q_on_way = shuffle_start([after(q_weight, kv_on_way[1])], place)
    kv = shuffle_end(kv_on_way[0], after(kv_on_way[1], hops["o"][1]), place)
    kv_half = kv.shape[1] // 2
    hops["k"], hops["v"] = [kv[:, :kv_half]], [kv[:, kv_half:]]
    pos = in_order(place % 2 == 0, pos_x, swap(pos_x, 1)).transpose(1, 0, 2).reshape(-1)
    hop("k")
    hop("v")
    q = shuffle_end(q_on_way[0], after(q_on_way[1], hops["k"][1]), place)
    q_half = q.shape[1] // 2
    hops["qa"], hops["qb"] = [q[:, :q_half]], [q[:, q_half:]]
    for name in ["k", "v"] * (planes - 2):
        hop(name, previous[-2])
    hop("qa", previous[-2])
    hop("qb", previous[-2])

    half = HEAD_SIZE // 2
    frequency = ROPE_BASE ** (-jnp.arange(half, dtype=jnp.float32) / half)
    angles = pos.astype(jnp.float32)[:, None] * frequency[None, :]
    cosine, sine = jnp.cos(angles), jnp.sin(angles)
    turn = (
        jnp.concatenate([cosine, cosine], axis=1),
        jnp.concatenate([-sine, sine], axis=1),
    )

    own_kv = project(
        after(normed, *turn),
        source,
        [hops["k"], hops["v"]],
        1,
        key_norm_gain,
        turn,
    )
    for n in range(planes - 2):
        hop("qa", own_kv)
        hop("qb", own_kv)
    up = [(c, c + 1) for c in range(planes - 1)]
    halo = lax.ppermute(own_kv[plane_tokens - VISIBLE_SPAN :], "z", up)
    all_kv = jnp.concatenate([halo, own_kv], axis=0)
    for _ in range(planes - 3):
        hop("o", previous[-2])

    factor = (MODEL_WIDTH // QUERY_HEADS) ** (-0.5)
    queries = [
        project(after(normed, own_kv), source, [hops[name]], 1, q_gain, turn, factor)
        for name in ("qa", "qb")
    ]

    own = [attend(0, pos[:, None], queries, all_kv)]
    own.append(attend(1, after(pos[:, None], own[0]), queries, all_kv))
    hop("o", own[0])
    per_side = planes // 2
    kept, slots = [], []
    for d in range(per_side):
        near, opposite = source[d], source[d + per_side]
        kept.append(jnp.where(near // per_side == side, 0, 1))
        which = jnp.where(kept[d] == 0, near, opposite) % per_side
        slots += [which * INNER + (place ^ mask) for mask in range(INNER)]
    slots = jnp.stack(slots).astype(jnp.int32)
    keeps, arrived = [], []
    pairs = [block for d in range(per_side) for block in (hops["o"][d], hops["o"][d + per_side])]
    for part in range(2):
        far = swap(own[part], 2)
        first = after(own[0], own[1]) if part == 0 else after(own[1], keeps[-1])
        across = after(far, own[1]) if part == 0 else after(far, keeps[-1], arrived[0])
        attended = [first, swap(own[part], 1), far, swap(across, 1)]
        terms = group_product(place, kept, attended, pairs)
        keeps += terms[::2]
        arrived += [swap_tp(give) for give in terms[1::2]]

    output = None
    for part in range(2):
        sums = []
        for n in range(part * per_side, (part + 1) * per_side):
            theirs = after(arrived[n], keeps[-1]) if part == 0 else arrived[n]
            total = keeps[n].astype(jnp.float32) + theirs.astype(jnp.float32)
            sums.append(total.astype(jnp.bfloat16))
        shipped = [jnp.concatenate(sums, axis=0)] if part == 0 else sums
        blocks = []
        for total in shipped:
            for mask in range(INNER):
                at = (place ^ mask) * QUERY_BLOCK
                block = lax.dynamic_slice_in_dim(total, at, QUERY_BLOCK, axis=1)
                blocks.append(swap(block, mask) if mask else block)
        if part == 0:
            height = sums[0].shape[0]
            blocks = [block[n * height : (n + 1) * height] for n in range(per_side) for block in blocks]
        squares = squares_of(blocks)
        output = finish(
            part, slots, squares, swap_tp(squares), post_gain, inputs, blocks, output
        )
    return output


def from_behind(x, axis, by):
    size = lax.axis_size(axis)
    pairs = [(i, i + by) for i in range(size) if 0 <= i + by < size]
    return lax.ppermute(x, axis, pairs)


def block_scores(grouped, keys_block):
    return jnp.einsum("qhgd,khd->hgqk", grouped, keys_block, preferred_element_type=jnp.float32)


def block_mix(weights_block, values_block):
    return jnp.einsum(
        "hgqk,khd->qhgd", weights_block, values_block, preferred_element_type=jnp.float32
    )


def gather_features(inputs):
    if lax.axis_size("tp") != 2:
        return lax.all_gather(inputs, "tp", axis=1, tiled=True)
    other = lax.ppermute(inputs, "tp", [(0, 1), (1, 0)])
    first = lax.axis_index("tp") == 0
    return jnp.concatenate(
        [jnp.where(first, inputs, other), jnp.where(first, other, inputs)], axis=1
    )


def project_out(attended, out_full):
    if lax.axis_size("tp") != 2:
        partial_terms = jnp.dot(attended, out_full, preferred_element_type=jnp.float32)
        return lax.psum_scatter(
            partial_terms.astype(jnp.bfloat16), "tp", scatter_dimension=1, tiled=True
        ).astype(jnp.float32)
    here = lax.axis_index("tp")
    cols = out_full.shape[1] // 2

    def half(which):
        weight = lax.dynamic_slice_in_dim(out_full, which * cols, cols, axis=1)
        return jnp.dot(attended, weight, preferred_element_type=jnp.float32).astype(jnp.bfloat16)

    theirs = half(1 - here)
    arrived = lax.ppermute(theirs, "tp", [(0, 1), (1, 0)])
    return half(here).astype(jnp.float32) + arrived.astype(jnp.float32)


def by_devices(
    inputs,
    in_gain,
    q_weight,
    key_matrix,
    value_matrix,
    q_gain,
    key_norm_gain,
    out_weight,
    post_gain,
    segment_ids,
    positions,
):
    tok_rows = inputs.shape[0]
    q_cols = q_weight.shape[1]
    kv_cols = key_matrix.shape[1]
    stacked = jnp.concatenate([key_matrix, value_matrix, q_weight], axis=1)
    weights_full = lax.all_gather(stacked, "ctx", axis=0, tiled=True)
    out_full = lax.all_gather(out_weight, "ctx", axis=1, tiled=True)
    gathered = gather_features(inputs)
    normalized = rms_scale(gathered.astype(jnp.float32), in_gain).astype(jnp.bfloat16)
    raw = jnp.dot(normalized, weights_full, preferred_element_type=jnp.float32)
    k_raw = raw[:, :kv_cols]
    v_raw = raw[:, kv_cols : 2 * kv_cols]
    q_raw = raw[:, 2 * kv_cols :]
    q_heads = q_cols // HEAD_SIZE
    kv_heads = kv_cols // HEAD_SIZE
    turn = angles_of(positions, HEAD_SIZE // 2)
    query_heads_all = prepare_heads(
        q_raw, q_gain, turn, (MODEL_WIDTH // QUERY_HEADS) ** (-0.5)
    )
    keys_own = prepare_heads(k_raw, key_norm_gain, turn, 1.0)
    keys_own = keys_own.reshape(tok_rows, kv_heads, HEAD_SIZE)
    values_own = v_raw.reshape(tok_rows, kv_heads, HEAD_SIZE).astype(jnp.bfloat16)
    reach = (VISIBLE_SPAN - 1) // tok_rows + 1
    key_list = [keys_own]
    value_list = [values_own]
    segment_list = [segment_ids]
    for distance in range(1, reach + 1):
        far_keys, far_values, far_segments = from_behind(
            (keys_own, values_own, segment_ids), "ctx", distance
        )
        key_list.insert(0, far_keys)
        value_list.insert(0, far_values)
        segment_list.insert(0, far_segments)
    key_all = jnp.concatenate(key_list, axis=0)
    value_all = jnp.concatenate(value_list, axis=0)
    segment_all = jnp.concatenate(segment_list, axis=0)
    my_start = lax.axis_index("ctx") * tok_rows
    key_index = my_start - reach * tok_rows + jnp.arange((reach + 1) * tok_rows, dtype=jnp.int32)
    query_index = my_start + jnp.arange(tok_rows, dtype=jnp.int32)
    gap = query_index[:, None] - key_index[None, :]
    allowed = (
        (segment_ids[:, None] == segment_all[None, :])
        & (gap >= 0)
        & (gap < VISIBLE_SPAN)
        & (key_index[None, :] >= 0)
    )
    head_group = q_heads // kv_heads
    grouped = query_heads_all.reshape(tok_rows, kv_heads, head_group, HEAD_SIZE)
    scores = block_scores(grouped, key_all)
    scores = jnp.where(allowed[None, None], scores, MASKED)
    expo = jnp.exp(scores - jnp.max(scores, axis=-1, keepdims=True))
    weights = (expo / jnp.sum(expo, axis=-1, keepdims=True)).astype(jnp.bfloat16)
    mixed = block_mix(weights, value_all)
    attended = mixed.reshape(tok_rows, q_cols).astype(jnp.bfloat16)
    share = project_out(attended, out_full)
    squares = lax.psum(jnp.sum(share * share, axis=-1), "tp")
    branch = share * lax.rsqrt(squares[:, None] / MODEL_WIDTH + EPS) * post_gain
    return (inputs.astype(jnp.float32) + branch).astype(jnp.bfloat16)


def solution(mesh):
    ctx, tp = mesh.shape["ctx"], mesh.shape["tp"]
    whole_planes = tp == 2 and ctx % (2 * INNER) == 0
    if whole_planes:
        devices = mesh.devices.reshape(ctx // INNER, INNER, tp)
        mesh = jax.sharding.Mesh(devices, ("z", "i", "tp"))
    tokens = ("z", "i") if whole_planes else "ctx"
    return jax.shard_map(
        by_planes if whole_planes else by_devices,
        mesh=mesh,
        in_specs=(
            P(tokens, "tp"),
            P(),
            P(tokens, "tp"),
            P(tokens, "tp"),
            P(tokens, "tp"),
            P(),
            P(),
            P("tp", tokens),
            P("tp"),
            P(tokens),
            P(tokens),
        ),
        out_specs=P(tokens, "tp"),
        check_vma=False,
    )
```

```python
import functools

import jax
import jax.numpy as jnp
from jax import lax
from jax.experimental import pallas as pl
from jax.experimental.pallas import tpu as pltpu
from jax.sharding import PartitionSpec as P

MODEL_WIDTH = 5376
QUERY_HEADS = 32
HEAD_SIZE = 128
VISIBLE_SPAN = 1024


EPS = 1e-06
ROPE_BASE = 10000.0
MASKED = -1e30

INNER = 4
QUERY_BLOCK = 256
TOKEN_BLOCK = 512
MIB = 2**20


def lasting(microseconds):
    return pl.CostEstimate(flops=int(microseconds * 1e9), bytes_accessed=0, transcendentals=0)


def rms_scale(values, gain):
    return values * lax.rsqrt(jnp.mean(values * values, axis=-1, keepdims=True) + EPS) * gain


def angles_of(position, half_dim):
    frequency = ROPE_BASE ** (-jnp.arange(half_dim, dtype=jnp.float32) / half_dim)
    angles = position.astype(jnp.float32)[:, None] * frequency[None, :]
    return jnp.cos(angles)[:, None, :], jnp.sin(angles)[:, None, :]


def rotate(values, cosine, sine):
    half_dim = values.shape[-1] // 2
    first = values[..., :half_dim]
    second = values[..., half_dim:]
    return jnp.concatenate(
        [first * cosine - second * sine, second * cosine + first * sine], axis=-1
    )


def prepare_heads(projected, gain, turn, factor):
    shaped = projected.reshape(projected.shape[0], -1, HEAD_SIZE)
    turned = rotate(rms_scale(shaped, gain), *turn) * factor
    return turned.astype(jnp.bfloat16).reshape(projected.shape)


def swap(x, mask):
    return lax.ppermute(x, "i", [(c, c ^ mask) for c in range(INNER)])


def swap_tp(x):
    return lax.ppermute(x, "tp", [(0, 1), (1, 0)])


def ring_step(x):
    size = lax.axis_size("z")
    return lax.ppermute(x, "z", [(c, (c + 1) % size) for c in range(size)])


def after(x, *others):
    return lax.optimization_barrier((x, *others))[0]


def in_order(first, mine, other):
    return jnp.where(first, jnp.stack([mine, other]), jnp.stack([other, mine]))


def project_kernel(factor, turned_cols, blocks, source_ref, x_ref, *refs):
    o_ref, whole_ref = refs[-2:]
    gain_ref, cos_ref, sin_ref = refs[-5:-2]
    weights = refs[:-5]

    @pl.when(pl.program_id(0) == 0)
    def _():
        for n, weight_ref in enumerate(weights):
            height, width = weight_ref.shape
            row = pl.multiple_of(source_ref[n % blocks] * height, 64)
            col = n // blocks * width
            whole_ref[pl.ds(row, height), col : col + width] = weight_ref[...]

    depth = x_ref.shape[-1]
    total = None
    for side in range(x_ref.shape[1]):
        term = jnp.dot(
            x_ref[0, side],
            whole_ref[side * depth : (side + 1) * depth, :],
            preferred_element_type=jnp.float32,
        )
        total = term if total is None else total + term
    for head in range(turned_cols // HEAD_SIZE):
        span = slice(head * HEAD_SIZE, (head + 1) * HEAD_SIZE)
        values = rms_scale(total[:, span], gain_ref[...])
        turned = pltpu.roll(values, HEAD_SIZE // 2, 1)
        values = values * cos_ref[...] + turned * sin_ref[...]
        o_ref[:, span] = (values * factor).astype(jnp.bfloat16)
    if turned_cols < total.shape[1]:
        o_ref[:, turned_cols:] = total[:, turned_cols:].astype(jnp.bfloat16)


def project(normed, source, groups, turned_groups, gain, turn, factor=1.0):
    inner, sides, rows, depth = normed.shape
    height, width = groups[0][0].shape
    cols = width * len(groups)
    weights = [block for group in groups for block in group]
    tokens = inner * rows
    return pl.pallas_call(
        functools.partial(project_kernel, factor, turned_groups * width, len(groups[0])),
        grid=(inner,),
        in_specs=[
            pl.BlockSpec(memory_space=pltpu.SMEM),
            pl.BlockSpec((1, sides, rows, depth), lambda b: (b, 0, 0, 0)),
        ]
        + [pl.BlockSpec((height, width), lambda b: (0, 0)) for _ in weights]
        + [pl.BlockSpec((1, HEAD_SIZE), lambda b: (0, 0))]
        + [pl.BlockSpec((rows, HEAD_SIZE), lambda b: (b, 0)) for _ in turn],
        out_specs=pl.BlockSpec((rows, cols), lambda b: (b, 0)),
        out_shape=jax.ShapeDtypeStruct((tokens, cols), jnp.bfloat16),
        scratch_shapes=[pltpu.VMEM((sides * depth, cols), jnp.bfloat16)],
        compiler_params=pltpu.CompilerParams(vmem_limit_bytes=36 * MIB),
        cost_estimate=lasting(width / 26),
    )(source, normed, *weights, gain.reshape(1, HEAD_SIZE), *turn)


def attend_kernel(part, pos_ref, *refs):
    queries, (kv_ref, o_ref) = refs[:-2], refs[-2:]
    start = pl.multiple_of((pl.program_id(0) * 2 + part) * QUERY_BLOCK, QUERY_BLOCK)
    window = VISIBLE_SPAN + QUERY_BLOCK
    shape = (QUERY_BLOCK, window)
    last = lax.broadcasted_iota(jnp.int32, shape, 0) + VISIBLE_SPAN
    column = lax.broadcasted_iota(jnp.int32, shape, 1)
    first = last - jnp.minimum(pos_ref[...], VISIBLE_SPAN - 1)
    allowed = (column <= last) & (column >= first)
    bias = jnp.where(allowed, 0.0, MASKED)
    tall = jnp.concatenate([bias, bias], axis=0)
    kv_heads = len(queries)
    for kv_head, q_ref in enumerate(queries):
        keys = kv_ref[pl.ds(start, window), pl.ds(kv_head * HEAD_SIZE, HEAD_SIZE)]
        values = kv_ref[pl.ds(start, window), pl.ds((kv_heads + kv_head) * HEAD_SIZE, HEAD_SIZE)]
        group = q_ref.shape[1] // HEAD_SIZE
        stacked = jnp.concatenate(
            [q_ref[:, h * HEAD_SIZE : (h + 1) * HEAD_SIZE] for h in range(group)], axis=0
        )
        scores = lax.dot_general(
            stacked, keys, (((1,), (1,)), ((), ())), preferred_element_type=jnp.float32
        )
        scores = scores + tall
        expo = jnp.exp(scores - jnp.max(scores, axis=-1, keepdims=True))
        weights = (expo * (1.0 / jnp.sum(expo, axis=-1, keepdims=True))).astype(jnp.bfloat16)
        mixed = jnp.dot(weights, values, preferred_element_type=jnp.float32).astype(jnp.bfloat16)
        for head in range(group):
            place = (kv_head * group + head) * HEAD_SIZE
            o_ref[:, place : place + HEAD_SIZE] = mixed[head * QUERY_BLOCK : (head + 1) * QUERY_BLOCK]


def attend(part, position, queries, all_kv):
    tokens, cols = queries[0].shape
    window = VISIBLE_SPAN + QUERY_BLOCK
    width = cols * len(queries)
    half = tokens // 2
    return pl.pallas_call(
        functools.partial(attend_kernel, part),
        grid=(half // QUERY_BLOCK,),
        in_specs=[pl.BlockSpec((QUERY_BLOCK, 1), lambda b: (2 * b + part, 0))]
        + [pl.BlockSpec((QUERY_BLOCK, cols), lambda b: (2 * b + part, 0)) for _ in queries]
        + [pl.BlockSpec(all_kv.shape, lambda b: (0, 0))],
        out_specs=pl.BlockSpec((QUERY_BLOCK, width), lambda b: (b, 0)),
        out_shape=jax.ShapeDtypeStruct((half, width), jnp.bfloat16),
        compiler_params=pltpu.CompilerParams(vmem_limit_bytes=20 * MIB),
        cost_estimate=lasting(14.5),
    )(position, *queries, all_kv)


def group_kernel(inner, place_ref, kept_ref, *refs):
    pairs = kept_ref.shape[0]
    lefts, weights, outs = refs[:inner], refs[inner : inner + 2 * pairs], refs[inner + 2 * pairs :]
    place = place_ref[0]
    depth = lefts[0].shape[1]
    for n, weight_ref in enumerate(weights):
        total = None
        for m in range(inner):
            row = pl.multiple_of((place ^ m) * depth, depth)
            term = lax.dot_general(
                weight_ref[:, pl.ds(row, depth)],
                lefts[m][...],
                (((1,), (1,)), ((), ())),
                preferred_element_type=jnp.float32,
            )
            total = term if total is None else total + term
        total = total.astype(jnp.bfloat16)
        kept = kept_ref[n // 2]
        for out, which in zip(outs[n // 2 * 2 : n // 2 * 2 + 2], (kept, 1 - kept)):

            @pl.when(which == n % 2)
            def _():
                out[...] = total


def group_product(place, kept, attended, weights):
    tokens, depth = attended[0].shape
    cols, rows = weights[0].shape
    shape = jax.ShapeDtypeStruct((cols, tokens), jnp.bfloat16)
    return pl.pallas_call(
        functools.partial(group_kernel, len(attended)),
        grid=(tokens // TOKEN_BLOCK,),
        in_specs=[pl.BlockSpec(memory_space=pltpu.SMEM)] * 2
        + [pl.BlockSpec((TOKEN_BLOCK, depth), lambda b: (b, 0)) for _ in attended]
        + [pl.BlockSpec((cols, rows), lambda b: (0, 0)) for _ in weights],
        out_specs=[pl.BlockSpec((cols, TOKEN_BLOCK), lambda b: (0, b))] * len(weights),
        out_shape=[shape] * len(weights),
        compiler_params=pltpu.CompilerParams(vmem_limit_bytes=24 * MIB),
        cost_estimate=lasting(2.9 * len(weights)),
    )(jnp.reshape(place, (1,)), jnp.stack(kept).astype(jnp.int32), *attended, *weights)


def squares_kernel(*refs):
    total = None
    for ref in refs[:-1]:
        values = ref[...].astype(jnp.float32)
        term = jnp.sum(values * values, axis=0, keepdims=True)
        total = term if total is None else total + term
    refs[-1][...] = total


def squares_of(blocks):
    return pl.pallas_call(
        squares_kernel,
        out_shape=jax.ShapeDtypeStruct((1, blocks[0].shape[1]), jnp.float32),
        compiler_params=pltpu.CompilerParams(vmem_limit_bytes=8 * MIB),
    )(*blocks)


def finish_kernel(count, slots_ref, own_ref, other_ref, gain_ref, input_ref, *refs):
    blocks, (o_ref, share_ref) = refs[:count], refs[-2:]
    height = blocks[0].shape[0]
    for n, block in enumerate(blocks):
        row = pl.multiple_of(slots_ref[n] * height, 16)
        share_ref[pl.ds(row, height), :] = block[...]
    scale = lax.rsqrt((own_ref[...] + other_ref[...]) / MODEL_WIDTH + EPS)
    for col in range(0, share_ref.shape[0], HEAD_SIZE):
        span = slice(col, col + HEAD_SIZE)
        branch = (share_ref[span, :].astype(jnp.float32) * scale).T * gain_ref[:, span]
        o_ref[:, span] = (input_ref[:, span].astype(jnp.float32) + branch).astype(jnp.bfloat16)


def finish(part, slots, own, other, gain, inputs, blocks, so_far):
    rows, cols = inputs.shape
    step = blocks[0].shape[1]
    whole = lambda x: pl.BlockSpec(x.shape, lambda b: (0, 0))
    extra = [] if so_far is None else [so_far]
    operands = [slots, own, other, gain.reshape(1, cols), inputs, *blocks, *extra]
    return pl.pallas_call(
        functools.partial(finish_kernel, len(blocks)),
        grid=(1,),
        in_specs=[pl.BlockSpec(memory_space=pltpu.SMEM), whole(own), whole(other), whole(operands[3])]
        + [pl.BlockSpec((step, cols), lambda b: (part, 0))]
        + [whole(block) for block in blocks]
        + [pl.BlockSpec(memory_space=pl.ANY) for _ in extra],
        out_specs=pl.BlockSpec((step, cols), lambda b: (part, 0)),
        out_shape=jax.ShapeDtypeStruct((rows, cols), jnp.bfloat16),
        scratch_shapes=[pltpu.VMEM((cols, step), jnp.bfloat16)],
        input_output_aliases={len(operands) - 1: 0} if extra else {},
        compiler_params=pltpu.CompilerParams(vmem_limit_bytes=16 * MIB),
    )(*operands)


def shuffle_start(weights, place):
    def cut(which):
        parts = []
        for core in range(2):
            cols = [w.shape[1] // INNER for w in weights]
            spans = [
                lax.dynamic_slice_in_dim(w, (which * 2 + core) * n, n, axis=1)
                for w, n in zip(weights, cols)
            ]
            parts.append(jnp.concatenate(spans, axis=1) if len(spans) > 1 else spans[0])
        return jnp.stack(parts)

    side = place // 2
    return cut(side), swap(cut(1 - side), 2)


def shuffle_end(mine, theirs, place):
    core = place % 2
    rows = in_order(place // 2 == 0, mine, theirs)
    keep = lax.dynamic_index_in_dim(rows, core, 1, keepdims=False)
    give = lax.dynamic_index_in_dim(rows, 1 - core, 1, keepdims=False)
    whole = in_order(core == 0, keep, swap(give, 1))
    return whole.transpose(1, 0, 2, 3).reshape(-1, whole.shape[-1])


def by_planes(
    inputs,
    in_gain,
    q_weight,
    key_matrix,
    value_matrix,
    q_gain,
    key_norm_gain,
    out_weight,
    post_gain,
    segment_ids,
    positions,
):
    tok_rows = inputs.shape[0]
    planes = lax.axis_size("z")
    place, plane, side = lax.axis_index("i"), lax.axis_index("z"), lax.axis_index("tp")
    plane_tokens = INNER * tok_rows
    source = ((plane - jnp.arange(planes)) % planes).astype(jnp.int32)

    kv_on_way = shuffle_start([key_matrix, value_matrix], place)
    out_rows = out_weight.T
    hops = {"o": [out_rows]}
    previous = []

    def hop(name, *others):
        block = hops[name][-1]
        hops[name].append(ring_step(after(block, *others) if others else block))
        previous.append(hops[name][-1])

    hop("o")
    values = inputs.astype(jnp.float32)
    squares = jnp.sum(values * values, axis=-1)
    scale = lax.rsqrt((squares + swap_tp(squares)) / MODEL_WIDTH + EPS)
    gain = lax.dynamic_slice_in_dim(in_gain, side * inputs.shape[1], inputs.shape[1])
    normed = (values * scale[:, None] * gain).astype(jnp.bfloat16)

    pos_x = in_order(place // 2 == 0, positions, swap(positions, 2))
    q_on_way = shuffle_start([after(q_weight, kv_on_way[1])], place)
    kv = shuffle_end(*kv_on_way, place)
    normed = lax.all_gather(after(normed, hops["o"][1], kv), ("i", "tp"), axis=0, tiled=False)
    normed = normed.reshape(INNER, 2, *inputs.shape)
    kv_half = kv.shape[1] // 2
    hops["k"], hops["v"] = [kv[:, :kv_half]], [kv[:, kv_half:]]
    pos = in_order(place % 2 == 0, pos_x, swap(pos_x, 1)).transpose(1, 0, 2).reshape(-1)
    hop("k")
    hop("v")
    q = shuffle_end(q_on_way[0], after(q_on_way[1], hops["k"][1]), place)
    q_half = q.shape[1] // 2
    hops["qa"], hops["qb"] = [q[:, :q_half]], [q[:, q_half:]]
    for name in ["k", "v"] * (planes - 2):
        hop(name, previous[-2])
    hop("qa", previous[-2])
    hop("qb", previous[-2])

    half = HEAD_SIZE // 2
    frequency = ROPE_BASE ** (-jnp.arange(half, dtype=jnp.float32) / half)
    angles = pos.astype(jnp.float32)[:, None] * frequency[None, :]
    cosine, sine = jnp.cos(angles), jnp.sin(angles)
    turn = (
        jnp.concatenate([cosine, cosine], axis=1),
        jnp.concatenate([-sine, sine], axis=1),
    )

    own_kv = project(
        after(normed, *turn),
        source,
        [hops["k"], hops["v"]],
        1,
        key_norm_gain,
        turn,
    )
    for n in range(planes - 2):
        hop("qa", *[own_kv][:n])
        hop("qb", *[own_kv][:n])
    up = [(c, c + 1) for c in range(planes - 1)]
    halo = lax.ppermute(own_kv[plane_tokens - VISIBLE_SPAN :], "z", up)
    all_kv = jnp.concatenate([halo, own_kv], axis=0)
    for _ in range(planes - 3):
        hop("o", previous[-2])

    factor = (MODEL_WIDTH // QUERY_HEADS) ** (-0.5)
    queries = [
        project(after(normed, own_kv), source, [hops[name]], 1, q_gain, turn, factor)
        for name in ("qa", "qb")
    ]

    own = [attend(0, pos[:, None], queries, all_kv)]
    own.append(attend(1, after(pos[:, None], own[0]), queries, all_kv))
    hop("o", own[0])
    per_side = planes // 2
    kept, slots = [], []
    for d in range(per_side):
        near, opposite = source[d], source[d + per_side]
        kept.append(jnp.where(near // per_side == side, 0, 1))
        which = jnp.where(kept[d] == 0, near, opposite) % per_side
        slots += [which * INNER + (place ^ mask) for mask in range(INNER)]
    slots = jnp.stack(slots).astype(jnp.int32)
    keeps, arrived = [], []
    pairs = [block for d in range(per_side) for block in (hops["o"][d], hops["o"][d + per_side])]
    for part in range(2):
        far = swap(own[part], 2)
        first = after(own[0], own[1]) if part == 0 else after(own[1], keeps[-1])
        across = after(far, own[1]) if part == 0 else after(far, keeps[-1], arrived[0])
        attended = [first, swap(own[part], 1), far, swap(across, 1)]
        terms = group_product(place, kept, attended, pairs)
        keeps += terms[::2]
        arrived += [swap_tp(give) for give in terms[1::2]]

    output = None
    for part in range(2):
        sums = []
        for n in range(part * per_side, (part + 1) * per_side):
            theirs = after(arrived[n], keeps[-1]) if part == 0 else arrived[n]
            total = keeps[n].astype(jnp.float32) + theirs.astype(jnp.float32)
            sums.append(total.astype(jnp.bfloat16))
        shipped = [jnp.concatenate(sums, axis=0)] if part == 0 else sums
        blocks = []
        for total in shipped:
            for mask in range(INNER):
                at = (place ^ mask) * QUERY_BLOCK
                block = lax.dynamic_slice_in_dim(total, at, QUERY_BLOCK, axis=1)
                blocks.append(swap(block, mask) if mask else block)
        if part == 0:
            height = sums[0].shape[0]
            blocks = [block[n * height : (n + 1) * height] for n in range(per_side) for block in blocks]
        squares = squares_of(blocks)
        output = finish(
            part, slots, squares, swap_tp(squares), post_gain, inputs, blocks, output
        )
    return output


def from_behind(x, axis, by):
    size = lax.axis_size(axis)
    pairs = [(i, i + by) for i in range(size) if 0 <= i + by < size]
    return lax.ppermute(x, axis, pairs)


def block_scores(grouped, keys_block):
    return jnp.einsum("qhgd,khd->hgqk", grouped, keys_block, preferred_element_type=jnp.float32)


def block_mix(weights_block, values_block):
    return jnp.einsum(
        "hgqk,khd->qhgd", weights_block, values_block, preferred_element_type=jnp.float32
    )


def gather_features(inputs):
    if lax.axis_size("tp") != 2:
        return lax.all_gather(inputs, "tp", axis=1, tiled=True)
    other = lax.ppermute(inputs, "tp", [(0, 1), (1, 0)])
    first = lax.axis_index("tp") == 0
    return jnp.concatenate(
        [jnp.where(first, inputs, other), jnp.where(first, other, inputs)], axis=1
    )


def project_out(attended, out_full):
    if lax.axis_size("tp") != 2:
        partial_terms = jnp.dot(attended, out_full, preferred_element_type=jnp.float32)
        return lax.psum_scatter(
            partial_terms.astype(jnp.bfloat16), "tp", scatter_dimension=1, tiled=True
        ).astype(jnp.float32)
    here = lax.axis_index("tp")
    cols = out_full.shape[1] // 2

    def half(which):
        weight = lax.dynamic_slice_in_dim(out_full, which * cols, cols, axis=1)
        return jnp.dot(attended, weight, preferred_element_type=jnp.float32).astype(jnp.bfloat16)

    theirs = half(1 - here)
    arrived = lax.ppermute(theirs, "tp", [(0, 1), (1, 0)])
    return half(here).astype(jnp.float32) + arrived.astype(jnp.float32)


def by_devices(
    inputs,
    in_gain,
    q_weight,
    key_matrix,
    value_matrix,
    q_gain,
    key_norm_gain,
    out_weight,
    post_gain,
    segment_ids,
    positions,
):
    tok_rows = inputs.shape[0]
    q_cols = q_weight.shape[1]
    kv_cols = key_matrix.shape[1]
    stacked = jnp.concatenate([key_matrix, value_matrix, q_weight], axis=1)
    weights_full = lax.all_gather(stacked, "ctx", axis=0, tiled=True)
    out_full = lax.all_gather(out_weight, "ctx", axis=1, tiled=True)
    gathered = gather_features(inputs)
    normalized = rms_scale(gathered.astype(jnp.float32), in_gain).astype(jnp.bfloat16)
    raw = jnp.dot(normalized, weights_full, preferred_element_type=jnp.float32)
    k_raw = raw[:, :kv_cols]
    v_raw = raw[:, kv_cols : 2 * kv_cols]
    q_raw = raw[:, 2 * kv_cols :]
    q_heads = q_cols // HEAD_SIZE
    kv_heads = kv_cols // HEAD_SIZE
    turn = angles_of(positions, HEAD_SIZE // 2)
    query_heads_all = prepare_heads(
        q_raw, q_gain, turn, (MODEL_WIDTH // QUERY_HEADS) ** (-0.5)
    )
    keys_own = prepare_heads(k_raw, key_norm_gain, turn, 1.0)
    keys_own = keys_own.reshape(tok_rows, kv_heads, HEAD_SIZE)
    values_own = v_raw.reshape(tok_rows, kv_heads, HEAD_SIZE).astype(jnp.bfloat16)
    reach = (VISIBLE_SPAN - 1) // tok_rows + 1
    key_list = [keys_own]
    value_list = [values_own]
    segment_list = [segment_ids]
    for distance in range(1, reach + 1):
        far_keys, far_values, far_segments = from_behind(
            (keys_own, values_own, segment_ids), "ctx", distance
        )
        key_list.insert(0, far_keys)
        value_list.insert(0, far_values)
        segment_list.insert(0, far_segments)
    key_all = jnp.concatenate(key_list, axis=0)
    value_all = jnp.concatenate(value_list, axis=0)
    segment_all = jnp.concatenate(segment_list, axis=0)
    my_start = lax.axis_index("ctx") * tok_rows
    key_index = my_start - reach * tok_rows + jnp.arange((reach + 1) * tok_rows, dtype=jnp.int32)
    query_index = my_start + jnp.arange(tok_rows, dtype=jnp.int32)
    gap = query_index[:, None] - key_index[None, :]
    allowed = (
        (segment_ids[:, None] == segment_all[None, :])
        & (gap >= 0)
        & (gap < VISIBLE_SPAN)
        & (key_index[None, :] >= 0)
    )
    head_group = q_heads // kv_heads
    grouped = query_heads_all.reshape(tok_rows, kv_heads, head_group, HEAD_SIZE)
    scores = block_scores(grouped, key_all)
    scores = jnp.where(allowed[None, None], scores, MASKED)
    expo = jnp.exp(scores - jnp.max(scores, axis=-1, keepdims=True))
    weights = (expo / jnp.sum(expo, axis=-1, keepdims=True)).astype(jnp.bfloat16)
    mixed = block_mix(weights, value_all)
    attended = mixed.reshape(tok_rows, q_cols).astype(jnp.bfloat16)
    share = project_out(attended, out_full)
    squares = lax.psum(jnp.sum(share * share, axis=-1), "tp")
    branch = share * lax.rsqrt(squares[:, None] / MODEL_WIDTH + EPS) * post_gain
    return (inputs.astype(jnp.float32) + branch).astype(jnp.bfloat16)


def solution(mesh):
    ctx, tp = mesh.shape["ctx"], mesh.shape["tp"]
    whole_planes = tp == 2 and ctx % (2 * INNER) == 0
    if whole_planes:
        devices = mesh.devices.reshape(ctx // INNER, INNER, tp)
        mesh = jax.sharding.Mesh(devices, ("z", "i", "tp"))
    tokens = ("z", "i") if whole_planes else "ctx"
    return jax.shard_map(
        by_planes if whole_planes else by_devices,
        mesh=mesh,
        in_specs=(
            P(tokens, "tp"),
            P(),
            P(tokens, "tp"),
            P(tokens, "tp"),
            P(tokens, "tp"),
            P(),
            P(),
            P("tp", tokens),
            P("tp"),
            P(tokens),
            P(tokens),
        ),
        out_specs=P(tokens, "tp"),
        check_vma=False,
    )
```

```python
import functools

import jax
import jax.numpy as jnp
from jax import lax
from jax.experimental import pallas as pl
from jax.experimental.pallas import tpu as pltpu
from jax.sharding import PartitionSpec as P

MODEL_WIDTH = 5376
QUERY_HEADS = 32
HEAD_SIZE = 128
VISIBLE_SPAN = 1024


EPS = 1e-06
ROPE_BASE = 10000.0
MASKED = -1e30

INNER = 4
QUERY_BLOCK = 256
TOKEN_BLOCK = 512
MIB = 2**20


def lasting(microseconds):
    return pl.CostEstimate(flops=int(microseconds * 1e9), bytes_accessed=0, transcendentals=0)


def rms_scale(values, gain):
    return values * lax.rsqrt(jnp.mean(values * values, axis=-1, keepdims=True) + EPS) * gain


def angles_of(position, half_dim):
    frequency = ROPE_BASE ** (-jnp.arange(half_dim, dtype=jnp.float32) / half_dim)
    angles = position.astype(jnp.float32)[:, None] * frequency[None, :]
    return jnp.cos(angles)[:, None, :], jnp.sin(angles)[:, None, :]


def rotate(values, cosine, sine):
    half_dim = values.shape[-1] // 2
    first = values[..., :half_dim]
    second = values[..., half_dim:]
    return jnp.concatenate(
        [first * cosine - second * sine, second * cosine + first * sine], axis=-1
    )


def prepare_heads(projected, gain, turn, factor):
    shaped = projected.reshape(projected.shape[0], -1, HEAD_SIZE)
    turned = rotate(rms_scale(shaped, gain), *turn) * factor
    return turned.astype(jnp.bfloat16).reshape(projected.shape)


def swap(x, mask):
    return lax.ppermute(x, "i", [(c, c ^ mask) for c in range(INNER)])


def swap_tp(x):
    return lax.ppermute(x, "tp", [(0, 1), (1, 0)])


def ring_step(x):
    size = lax.axis_size("z")
    return lax.ppermute(x, "z", [(c, (c + 1) % size) for c in range(size)])


def after(x, *others):
    return lax.optimization_barrier((x, *others))[0]


def in_order(first, mine, other):
    return jnp.where(first, jnp.stack([mine, other]), jnp.stack([other, mine]))


def project_kernel(factor, turned_cols, blocks, source_ref, x_ref, *refs):
    o_ref, whole_ref = refs[-2:]
    gain_ref, turn_ref = refs[-4:-2]
    weights = refs[:-4]

    @pl.when(pl.program_id(0) == 0)
    def _():
        for n, weight_ref in enumerate(weights):
            height, width = weight_ref.shape
            row = pl.multiple_of(source_ref[n % blocks] * height, 64)
            col = n // blocks * width
            whole_ref[pl.ds(row, height), col : col + width] = weight_ref[...]

    depth = x_ref.shape[-1]
    total = None
    for side in range(x_ref.shape[1]):
        term = jnp.dot(
            x_ref[0, side],
            whole_ref[side * depth : (side + 1) * depth, :],
            preferred_element_type=jnp.float32,
        )
        total = term if total is None else total + term
    here, there = turn_ref[...], pltpu.roll(turn_ref[...], HEAD_SIZE // 2, 1)
    first = lax.broadcasted_iota(jnp.int32, here.shape, 1) < HEAD_SIZE // 2
    cosine, sine = jnp.where(first, here, there), jnp.where(first, -there, here)
    for head in range(turned_cols // HEAD_SIZE):
        span = slice(head * HEAD_SIZE, (head + 1) * HEAD_SIZE)
        values = rms_scale(total[:, span], gain_ref[...])
        turned = pltpu.roll(values, HEAD_SIZE // 2, 1)
        values = values * cosine + turned * sine
        o_ref[:, span] = (values * factor).astype(jnp.bfloat16)
    if turned_cols < total.shape[1]:
        o_ref[:, turned_cols:] = total[:, turned_cols:].astype(jnp.bfloat16)


def project(normed, source, groups, turned_groups, gain, turn, factor=1.0):
    inner, sides, rows, depth = normed.shape
    height, width = groups[0][0].shape
    cols = width * len(groups)
    weights = [block for group in groups for block in group]
    tokens = inner * rows
    return pl.pallas_call(
        functools.partial(project_kernel, factor, turned_groups * width, len(groups[0])),
        grid=(inner,),
        in_specs=[
            pl.BlockSpec(memory_space=pltpu.SMEM),
            pl.BlockSpec((1, sides, rows, depth), lambda b: (b, 0, 0, 0)),
        ]
        + [pl.BlockSpec((height, width), lambda b: (0, 0)) for _ in weights]
        + [pl.BlockSpec((1, HEAD_SIZE), lambda b: (0, 0))]
        + [pl.BlockSpec((rows, HEAD_SIZE), lambda b: (b, 0))],
        out_specs=pl.BlockSpec((rows, cols), lambda b: (b, 0)),
        out_shape=jax.ShapeDtypeStruct((tokens, cols), jnp.bfloat16),
        scratch_shapes=[pltpu.VMEM((sides * depth, cols), jnp.bfloat16)],
        compiler_params=pltpu.CompilerParams(vmem_limit_bytes=36 * MIB),
        cost_estimate=lasting(width / 26),
    )(source, normed, *weights, gain.reshape(1, HEAD_SIZE), turn)


def attend_kernel(part, pos_ref, *refs):
    queries, (kv_ref, o_ref) = refs[:-2], refs[-2:]
    start = pl.multiple_of((pl.program_id(0) * 2 + part) * QUERY_BLOCK, QUERY_BLOCK)
    window = VISIBLE_SPAN + QUERY_BLOCK
    shape = (QUERY_BLOCK, window)
    last = lax.broadcasted_iota(jnp.int32, shape, 0) + VISIBLE_SPAN
    column = lax.broadcasted_iota(jnp.int32, shape, 1)
    first = last - jnp.minimum(pos_ref[...], VISIBLE_SPAN - 1)
    allowed = (column <= last) & (column >= first)
    bias = jnp.where(allowed, 0.0, MASKED)
    tall = jnp.concatenate([bias, bias], axis=0)
    kv_heads = len(queries)
    for kv_head, q_ref in enumerate(queries):
        keys = kv_ref[pl.ds(start, window), pl.ds(kv_head * HEAD_SIZE, HEAD_SIZE)]
        values = kv_ref[pl.ds(start, window), pl.ds((kv_heads + kv_head) * HEAD_SIZE, HEAD_SIZE)]
        group = q_ref.shape[1] // HEAD_SIZE
        stacked = jnp.concatenate(
            [q_ref[:, h * HEAD_SIZE : (h + 1) * HEAD_SIZE] for h in range(group)], axis=0
        )
        scores = lax.dot_general(
            stacked, keys, (((1,), (1,)), ((), ())), preferred_element_type=jnp.float32
        )
        scores = scores + tall
        expo = jnp.exp(scores - jnp.max(scores, axis=-1, keepdims=True))
        weights = (expo * (1.0 / jnp.sum(expo, axis=-1, keepdims=True))).astype(jnp.bfloat16)
        mixed = jnp.dot(weights, values, preferred_element_type=jnp.float32).astype(jnp.bfloat16)
        for head in range(group):
            place = (kv_head * group + head) * HEAD_SIZE
            o_ref[:, place : place + HEAD_SIZE] = mixed[head * QUERY_BLOCK : (head + 1) * QUERY_BLOCK]


def attend(part, position, queries, all_kv):
    tokens, cols = queries[0].shape
    window = VISIBLE_SPAN + QUERY_BLOCK
    width = cols * len(queries)
    half = tokens // 2
    return pl.pallas_call(
        functools.partial(attend_kernel, part),
        grid=(half // QUERY_BLOCK,),
        in_specs=[pl.BlockSpec((QUERY_BLOCK, 1), lambda b: (2 * b + part, 0))]
        + [pl.BlockSpec((QUERY_BLOCK, cols), lambda b: (2 * b + part, 0)) for _ in queries]
        + [pl.BlockSpec(all_kv.shape, lambda b: (0, 0))],
        out_specs=pl.BlockSpec((QUERY_BLOCK, width), lambda b: (b, 0)),
        out_shape=jax.ShapeDtypeStruct((half, width), jnp.bfloat16),
        compiler_params=pltpu.CompilerParams(vmem_limit_bytes=20 * MIB),
        cost_estimate=lasting(14.5),
    )(position, *queries, all_kv)


def group_kernel(inner, planes, pairs, facts_ref, *refs):
    lefts, weights, outs = refs[:inner], refs[inner : -2 * len(pairs)], refs[-2 * len(pairs) :]
    place = facts_ref[planes]
    depth = lefts[0].shape[1]
    for n, weight_ref in enumerate(weights):
        total = None
        for m in range(inner):
            row = pl.multiple_of((place ^ m) * depth, depth)
            term = lax.dot_general(
                weight_ref[:, pl.ds(row, depth)],
                lefts[m][...],
                (((1,), (1,)), ((), ())),
                preferred_element_type=jnp.float32,
            )
            total = term if total is None else total + term
        total = total.astype(jnp.bfloat16)
        kept = facts_ref[planes + 1 + pairs[n // 2]]
        for out, which in zip(outs[n // 2 * 2 :], (kept, 1 - kept)):

            @pl.when(which == n % 2)
            def _():
                out[...] = total


def group_product(facts, attended, blocks, pairs):
    tokens, depth = attended[0].shape
    cols, rows = blocks[0].shape
    weights = [blocks[n] for pair in pairs for n in (pair, pair + len(blocks) // 2)]
    shape = jax.ShapeDtypeStruct((cols, tokens), jnp.bfloat16)
    outs = pl.pallas_call(
        functools.partial(group_kernel, len(attended), len(blocks), pairs),
        grid=(tokens // TOKEN_BLOCK,),
        in_specs=[pl.BlockSpec(memory_space=pltpu.SMEM)]
        + [pl.BlockSpec((TOKEN_BLOCK, depth), lambda b: (b, 0)) for _ in attended]
        + [pl.BlockSpec((cols, rows), lambda b: (0, 0)) for _ in weights],
        out_specs=[pl.BlockSpec((cols, TOKEN_BLOCK), lambda b: (0, b))] * len(weights),
        out_shape=[shape] * len(weights),
        compiler_params=pltpu.CompilerParams(vmem_limit_bytes=24 * MIB),
        cost_estimate=lasting(2.9 * len(weights)),
    )(facts, *attended, *weights)
    return outs[::2], outs[1::2]


def squares_kernel(*refs):
    total = None
    for ref in refs[:-1]:
        values = ref[...].astype(jnp.float32)
        term = jnp.sum(values * values, axis=0, keepdims=True)
        total = term if total is None else total + term
    refs[-1][...] = total


def squares_of(blocks):
    return pl.pallas_call(
        squares_kernel,
        out_shape=jax.ShapeDtypeStruct((1, blocks[0].shape[1]), jnp.float32),
        compiler_params=pltpu.CompilerParams(vmem_limit_bytes=8 * MIB),
    )(*blocks)


def finish_kernel(inner, planes, facts_ref, own_ref, other_ref, gain_ref, input_ref, *refs):
    o_ref, share_ref = refs[-2:]
    place = facts_ref[planes]
    pairs = planes // 2
    height = share_ref.shape[0] // (pairs * inner)
    pair = 0
    while pair < pairs:
        spread, refs = refs[:inner], refs[inner:]
        for m, ref in enumerate(spread):
            for n in range(ref.shape[0] // height):
                slot = facts_ref[planes + 1 + pairs + pair + n] * inner + (place ^ m)
                row = pl.multiple_of(slot * height, 16)
                share_ref[pl.ds(row, height), :] = ref[n * height : (n + 1) * height, :]
        pair += spread[0].shape[0] // height
    scale = lax.rsqrt((own_ref[...] + other_ref[...]) / MODEL_WIDTH + EPS)
    for col in range(0, share_ref.shape[0], HEAD_SIZE):
        span = slice(col, col + HEAD_SIZE)
        branch = (share_ref[span, :].astype(jnp.float32) * scale).T * gain_ref[:, span]
        o_ref[:, span] = (input_ref[:, span].astype(jnp.float32) + branch).astype(jnp.bfloat16)


def finish(part, planes, facts, own, other, gain, inputs, spread, so_far):
    rows, cols = inputs.shape
    step = own.shape[1]
    whole = lambda x: pl.BlockSpec(x.shape, lambda b: (0, 0))
    extra = [] if so_far is None else [so_far]
    gain = gain.reshape(1, cols)
    operands = [facts, own, other, gain, inputs, *spread, *extra]
    return pl.pallas_call(
        functools.partial(finish_kernel, INNER, planes),
        grid=(1,),
        in_specs=[pl.BlockSpec(memory_space=pltpu.SMEM), whole(own), whole(other), whole(gain)]
        + [pl.BlockSpec((step, cols), lambda b: (part, 0))]
        + [whole(block) for block in spread]
        + [pl.BlockSpec(memory_space=pl.ANY) for _ in extra],
        out_specs=pl.BlockSpec((step, cols), lambda b: (part, 0)),
        out_shape=jax.ShapeDtypeStruct((rows, cols), jnp.bfloat16),
        scratch_shapes=[pltpu.VMEM((cols, step), jnp.bfloat16)],
        input_output_aliases={len(operands) - 1: 0} if extra else {},
        compiler_params=pltpu.CompilerParams(vmem_limit_bytes=16 * MIB),
        cost_estimate=lasting(2.5),
    )(*operands)


def shuffle_start(weights, place):
    def cut(which):
        parts = []
        for core in range(2):
            cols = [w.shape[1] // INNER for w in weights]
            spans = [
                lax.dynamic_slice_in_dim(w, (which * 2 + core) * n, n, axis=1)
                for w, n in zip(weights, cols)
            ]
            parts.append(jnp.concatenate(spans, axis=1) if len(spans) > 1 else spans[0])
        return jnp.stack(parts)

    side = place // 2
    return cut(side), swap(cut(1 - side), 2)


def shuffle_end(mine, theirs, place):
    core = place % 2
    rows = in_order(place // 2 == 0, mine, theirs)
    keep = lax.dynamic_index_in_dim(rows, core, 1, keepdims=False)
    give = lax.dynamic_index_in_dim(rows, 1 - core, 1, keepdims=False)
    whole = in_order(core == 0, keep, swap(give, 1))
    return whole.transpose(1, 0, 2, 3).reshape(-1, whole.shape[-1])


def by_planes(
    inputs,
    in_gain,
    q_weight,
    key_matrix,
    value_matrix,
    q_gain,
    key_norm_gain,
    out_weight,
    post_gain,
    segment_ids,
    positions,
):
    tok_rows = inputs.shape[0]
    planes = lax.axis_size("z")
    place, plane, side = lax.axis_index("i"), lax.axis_index("z"), lax.axis_index("tp")
    plane_tokens = INNER * tok_rows
    per_side = planes // 2
    source = [(plane - d) % planes for d in range(planes)]
    kept, slots = [], []
    for d in range(per_side):
        near, opposite = source[d], source[d + per_side]
        kept.append(jnp.where(near // per_side == side, 0, 1))
        slots.append(jnp.where(kept[d] == 0, near, opposite) % per_side)
    facts = jnp.stack([*source, place, *kept, *slots]).astype(jnp.int32)

    kv_on_way = shuffle_start([key_matrix, value_matrix], place)
    out_rows = out_weight.T
    hops = {"o": [out_rows]}
    previous = []

    def hop(name, *others):
        block = hops[name][-1]
        hops[name].append(ring_step(after(block, *others) if others else block))
        previous.append(hops[name][-1])

    hop("o")
    values = inputs.astype(jnp.float32)
    squares = jnp.sum(values * values, axis=-1)
    scale = lax.rsqrt((squares + swap_tp(squares)) / MODEL_WIDTH + EPS)
    gain = lax.dynamic_slice_in_dim(in_gain, side * inputs.shape[1], inputs.shape[1])
    normed = (values * scale[:, None] * gain).astype(jnp.bfloat16)

    pos_x = in_order(place // 2 == 0, positions, swap(positions, 2))
    q_on_way = shuffle_start([after(q_weight, kv_on_way[1])], place)
    kv = shuffle_end(*kv_on_way, place)
    normed = lax.all_gather(after(normed, hops["o"][1], kv), ("i", "tp"), axis=0, tiled=False)
    normed = normed.reshape(INNER, 2, *inputs.shape)
    kv_half = kv.shape[1] // 2
    hops["k"], hops["v"] = [kv[:, :kv_half]], [kv[:, kv_half:]]
    pos = in_order(place % 2 == 0, pos_x, swap(pos_x, 1)).transpose(1, 0, 2).reshape(-1)
    hop("k")
    hop("v")
    q = shuffle_end(q_on_way[0], after(q_on_way[1], hops["k"][1]), place)
    q_half = q.shape[1] // 2
    hops["qa"], hops["qb"] = [q[:, :q_half]], [q[:, q_half:]]
    for name in ["k", "v"] * (planes - 2):
        hop(name, previous[-2])
    hop("qa", previous[-2])
    hop("qb", previous[-2])

    half = HEAD_SIZE // 2
    frequency = ROPE_BASE ** (-jnp.arange(half, dtype=jnp.float32) / half)
    angles = pos.astype(jnp.float32)[:, None] * frequency[None, :]
    turn = jnp.concatenate([jnp.cos(angles), jnp.sin(angles)], axis=1)

    own_kv = project(
        after(normed, turn),
        facts,
        [hops["k"], hops["v"]],
        1,
        key_norm_gain,
        turn,
    )
    for n in range(planes - 2):
        hop("qa", *[own_kv][:n])
        hop("qb", *[own_kv][:n])
    up = [(c, c + 1) for c in range(planes - 1)]
    halo = lax.ppermute(own_kv[plane_tokens - VISIBLE_SPAN :], "z", up)
    all_kv = jnp.concatenate([halo, own_kv], axis=0)
    for _ in range(planes - 3):
        hop("o", previous[-2])

    factor = (MODEL_WIDTH // QUERY_HEADS) ** (-0.5)
    queries = [
        project(after(normed, own_kv), facts, [hops[name]], 1, q_gain, turn, factor)
        for name in ("qa", "qb")
    ]

    own = [attend(0, pos[:, None], queries, all_kv)]
    own.append(attend(1, pos[:, None], [after(queries[0], own[0], hops["o"][planes - 2]), queries[1]], all_kv))
    hop("o", own[0])
    keeps, arrived = [], []
    for part in range(2):
        far = swap(own[part], 2)
        first = after(own[0], own[1]) if part == 0 else after(own[1], keeps[-1])
        across = after(far, own[1] if part == 0 else keeps[-1])
        attended = [first, swap(own[part], 1), far, swap(across, 1)]
        for pairs in [range(per_side)]:
            kept_terms, given_terms = group_product(facts, attended, hops["o"], tuple(pairs))
            keeps += kept_terms
            arrived += [swap_tp(term) for term in given_terms]

    def to_tokens(total):
        blocks = []
        for mask in range(INNER):
            at = (place ^ mask) * QUERY_BLOCK
            block = lax.dynamic_slice_in_dim(total, at, QUERY_BLOCK, axis=1)
            blocks.append(swap(block, mask) if mask else block)
        return blocks

    output = None
    for part in range(2):
        sums, spread = [], []
        for n in range(part * per_side, (part + 1) * per_side):
            theirs = after(arrived[n], *(keeps[-1:] if part == 0 else spread[-INNER + 1 :]))
            total = keeps[n].astype(jnp.float32) + theirs.astype(jnp.float32)
            sums.append(total.astype(jnp.bfloat16))
            if part == 1:
                spread += to_tokens(sums[-1])
        if part == 0:
            spread = to_tokens(jnp.concatenate(sums, axis=0))
        if output is not None:
            spread[-1] = after(spread[-1], output)
        squares = squares_of(spread)
        output = finish(
            part, planes, facts, squares, swap_tp(squares), post_gain, inputs, spread, output
        )
    return output


def from_behind(x, axis, by):
    size = lax.axis_size(axis)
    pairs = [(i, i + by) for i in range(size) if 0 <= i + by < size]
    return lax.ppermute(x, axis, pairs)


def block_scores(grouped, keys_block):
    return jnp.einsum("qhgd,khd->hgqk", grouped, keys_block, preferred_element_type=jnp.float32)


def block_mix(weights_block, values_block):
    return jnp.einsum(
        "hgqk,khd->qhgd", weights_block, values_block, preferred_element_type=jnp.float32
    )


def gather_features(inputs):
    if lax.axis_size("tp") != 2:
        return lax.all_gather(inputs, "tp", axis=1, tiled=True)
    other = lax.ppermute(inputs, "tp", [(0, 1), (1, 0)])
    first = lax.axis_index("tp") == 0
    return jnp.concatenate(
        [jnp.where(first, inputs, other), jnp.where(first, other, inputs)], axis=1
    )


def project_out(attended, out_full):
    if lax.axis_size("tp") != 2:
        partial_terms = jnp.dot(attended, out_full, preferred_element_type=jnp.float32)
        return lax.psum_scatter(
            partial_terms.astype(jnp.bfloat16), "tp", scatter_dimension=1, tiled=True
        ).astype(jnp.float32)
    here = lax.axis_index("tp")
    cols = out_full.shape[1] // 2

    def half(which):
        weight = lax.dynamic_slice_in_dim(out_full, which * cols, cols, axis=1)
        return jnp.dot(attended, weight, preferred_element_type=jnp.float32).astype(jnp.bfloat16)

    theirs = half(1 - here)
    arrived = lax.ppermute(theirs, "tp", [(0, 1), (1, 0)])
    return half(here).astype(jnp.float32) + arrived.astype(jnp.float32)


def by_devices(
    inputs,
    in_gain,
    q_weight,
    key_matrix,
    value_matrix,
    q_gain,
    key_norm_gain,
    out_weight,
    post_gain,
    segment_ids,
    positions,
):
    tok_rows = inputs.shape[0]
    q_cols = q_weight.shape[1]
    kv_cols = key_matrix.shape[1]
    stacked = jnp.concatenate([key_matrix, value_matrix, q_weight], axis=1)
    weights_full = lax.all_gather(stacked, "ctx", axis=0, tiled=True)
    out_full = lax.all_gather(out_weight, "ctx", axis=1, tiled=True)
    gathered = gather_features(inputs)
    normalized = rms_scale(gathered.astype(jnp.float32), in_gain).astype(jnp.bfloat16)
    raw = jnp.dot(normalized, weights_full, preferred_element_type=jnp.float32)
    k_raw = raw[:, :kv_cols]
    v_raw = raw[:, kv_cols : 2 * kv_cols]
    q_raw = raw[:, 2 * kv_cols :]
    q_heads = q_cols // HEAD_SIZE
    kv_heads = kv_cols // HEAD_SIZE
    turn = angles_of(positions, HEAD_SIZE // 2)
    query_heads_all = prepare_heads(
        q_raw, q_gain, turn, (MODEL_WIDTH // QUERY_HEADS) ** (-0.5)
    )
    keys_own = prepare_heads(k_raw, key_norm_gain, turn, 1.0)
    keys_own = keys_own.reshape(tok_rows, kv_heads, HEAD_SIZE)
    values_own = v_raw.reshape(tok_rows, kv_heads, HEAD_SIZE).astype(jnp.bfloat16)
    reach = (VISIBLE_SPAN - 1) // tok_rows + 1
    key_list = [keys_own]
    value_list = [values_own]
    segment_list = [segment_ids]
    for distance in range(1, reach + 1):
        far_keys, far_values, far_segments = from_behind(
            (keys_own, values_own, segment_ids), "ctx", distance
        )
        key_list.insert(0, far_keys)
        value_list.insert(0, far_values)
        segment_list.insert(0, far_segments)
    key_all = jnp.concatenate(key_list, axis=0)
    value_all = jnp.concatenate(value_list, axis=0)
    segment_all = jnp.concatenate(segment_list, axis=0)
    my_start = lax.axis_index("ctx") * tok_rows
    key_index = my_start - reach * tok_rows + jnp.arange((reach + 1) * tok_rows, dtype=jnp.int32)
    query_index = my_start + jnp.arange(tok_rows, dtype=jnp.int32)
    gap = query_index[:, None] - key_index[None, :]
    allowed = (
        (segment_ids[:, None] == segment_all[None, :])
        & (gap >= 0)
        & (gap < VISIBLE_SPAN)
        & (key_index[None, :] >= 0)
    )
    head_group = q_heads // kv_heads
    grouped = query_heads_all.reshape(tok_rows, kv_heads, head_group, HEAD_SIZE)
    scores = block_scores(grouped, key_all)
    scores = jnp.where(allowed[None, None], scores, MASKED)
    expo = jnp.exp(scores - jnp.max(scores, axis=-1, keepdims=True))
    weights = (expo / jnp.sum(expo, axis=-1, keepdims=True)).astype(jnp.bfloat16)
    mixed = block_mix(weights, value_all)
    attended = mixed.reshape(tok_rows, q_cols).astype(jnp.bfloat16)
    share = project_out(attended, out_full)
    squares = lax.psum(jnp.sum(share * share, axis=-1), "tp")
    branch = share * lax.rsqrt(squares[:, None] / MODEL_WIDTH + EPS) * post_gain
    return (inputs.astype(jnp.float32) + branch).astype(jnp.bfloat16)


def solution(mesh):
    ctx, tp = mesh.shape["ctx"], mesh.shape["tp"]
    whole_planes = tp == 2 and ctx % (2 * INNER) == 0
    if whole_planes:
        devices = mesh.devices.reshape(ctx // INNER, INNER, tp)
        mesh = jax.sharding.Mesh(devices, ("z", "i", "tp"))
    tokens = ("z", "i") if whole_planes else "ctx"
    return jax.shard_map(
        by_planes if whole_planes else by_devices,
        mesh=mesh,
        in_specs=(
            P(tokens, "tp"),
            P(),
            P(tokens, "tp"),
            P(tokens, "tp"),
            P(tokens, "tp"),
            P(),
            P(),
            P("tp", tokens),
            P("tp"),
            P(tokens),
            P(tokens),
        ),
        out_specs=P(tokens, "tp"),
        check_vma=False,
    )
```

```python
import functools

import jax
import jax.numpy as jnp
from jax import lax
from jax.experimental import pallas as pl
from jax.experimental.pallas import tpu as pltpu
from jax.sharding import PartitionSpec as P

MODEL_WIDTH = 5376
QUERY_HEADS = 32
HEAD_SIZE = 128
VISIBLE_SPAN = 1024


EPS = 1e-06
ROPE_BASE = 10000.0
MASKED = -1e30

INNER = 4
QUERY_BLOCK = 256
TOKEN_BLOCK = 512
MIB = 2**20


def lasting(microseconds):
    return pl.CostEstimate(flops=int(microseconds * 1e9), bytes_accessed=0, transcendentals=0)


def rms_scale(values, gain):
    return values * lax.rsqrt(jnp.mean(values * values, axis=-1, keepdims=True) + EPS) * gain


def angles_of(position, half_dim):
    frequency = ROPE_BASE ** (-jnp.arange(half_dim, dtype=jnp.float32) / half_dim)
    angles = position.astype(jnp.float32)[:, None] * frequency[None, :]
    return jnp.cos(angles)[:, None, :], jnp.sin(angles)[:, None, :]


def rotate(values, cosine, sine):
    half_dim = values.shape[-1] // 2
    first = values[..., :half_dim]
    second = values[..., half_dim:]
    return jnp.concatenate(
        [first * cosine - second * sine, second * cosine + first * sine], axis=-1
    )


def prepare_heads(projected, gain, turn, factor):
    shaped = projected.reshape(projected.shape[0], -1, HEAD_SIZE)
    turned = rotate(rms_scale(shaped, gain), *turn) * factor
    return turned.astype(jnp.bfloat16).reshape(projected.shape)


def swap(x, mask):
    return lax.ppermute(x, "i", [(c, c ^ mask) for c in range(INNER)])


def swap_tp(x):
    return lax.ppermute(x, "tp", [(0, 1), (1, 0)])


def ring_step(x):
    size = lax.axis_size("z")
    return lax.ppermute(x, "z", [(c, (c + 1) % size) for c in range(size)])


def after(x, *others):
    return lax.optimization_barrier((x, *others))[0]


def in_order(first, mine, other):
    return jnp.where(first, jnp.stack([mine, other]), jnp.stack([other, mine]))


def project_kernel(factor, turned_cols, blocks, source_ref, x_ref, *refs):
    o_ref, whole_ref = refs[-2:]
    gain_ref, turn_ref = refs[-4:-2]
    weights = refs[:-4]

    @pl.when(pl.program_id(0) == 0)
    def _():
        for n, weight_ref in enumerate(weights):
            height, width = weight_ref.shape
            row = pl.multiple_of(source_ref[n % blocks] * height, 64)
            col = n // blocks * width
            whole_ref[pl.ds(row, height), col : col + width] = weight_ref[...]

    depth = x_ref.shape[-1]
    total = None
    for side in range(x_ref.shape[1]):
        term = jnp.dot(
            x_ref[0, side],
            whole_ref[side * depth : (side + 1) * depth, :],
            preferred_element_type=jnp.float32,
        )
        total = term if total is None else total + term
    here, there = turn_ref[...], pltpu.roll(turn_ref[...], HEAD_SIZE // 2, 1)
    first = lax.broadcasted_iota(jnp.int32, here.shape, 1) < HEAD_SIZE // 2
    cosine, sine = jnp.where(first, here, there), jnp.where(first, -there, here)
    for head in range(turned_cols // HEAD_SIZE):
        span = slice(head * HEAD_SIZE, (head + 1) * HEAD_SIZE)
        values = rms_scale(total[:, span], gain_ref[...])
        turned = pltpu.roll(values, HEAD_SIZE // 2, 1)
        values = values * cosine + turned * sine
        o_ref[:, span] = (values * factor).astype(jnp.bfloat16)
    if turned_cols < total.shape[1]:
        o_ref[:, turned_cols:] = total[:, turned_cols:].astype(jnp.bfloat16)


def project(normed, source, groups, turned_groups, gain, turn, factor=1.0):
    inner, sides, rows, depth = normed.shape
    height, width = groups[0][0].shape
    cols = width * len(groups)
    weights = [block for group in groups for block in group]
    tokens = inner * rows
    return pl.pallas_call(
        functools.partial(project_kernel, factor, turned_groups * width, len(groups[0])),
        grid=(inner,),
        in_specs=[
            pl.BlockSpec(memory_space=pltpu.SMEM),
            pl.BlockSpec((1, sides, rows, depth), lambda b: (b, 0, 0, 0)),
        ]
        + [pl.BlockSpec((height, width), lambda b: (0, 0)) for _ in weights]
        + [pl.BlockSpec((1, HEAD_SIZE), lambda b: (0, 0))]
        + [pl.BlockSpec((rows, HEAD_SIZE), lambda b: (b, 0))],
        out_specs=pl.BlockSpec((rows, cols), lambda b: (b, 0)),
        out_shape=jax.ShapeDtypeStruct((tokens, cols), jnp.bfloat16),
        scratch_shapes=[pltpu.VMEM((sides * depth, cols), jnp.bfloat16)],
        compiler_params=pltpu.CompilerParams(vmem_limit_bytes=36 * MIB),
        cost_estimate=lasting(width / 26),
    )(source, normed, *weights, gain.reshape(1, HEAD_SIZE), turn)


def attend_kernel(part, pos_ref, *refs):
    queries, (kv_ref, o_ref) = refs[:-2], refs[-2:]
    start = pl.multiple_of((pl.program_id(0) * 2 + part) * QUERY_BLOCK, QUERY_BLOCK)
    window = VISIBLE_SPAN + QUERY_BLOCK
    shape = (QUERY_BLOCK, window)
    last = lax.broadcasted_iota(jnp.int32, shape, 0) + VISIBLE_SPAN
    column = lax.broadcasted_iota(jnp.int32, shape, 1)
    first = last - jnp.minimum(pos_ref[...], VISIBLE_SPAN - 1)
    allowed = (column <= last) & (column >= first)
    bias = jnp.where(allowed, 0.0, MASKED)
    tall = jnp.concatenate([bias, bias], axis=0)
    kv_heads = len(queries)
    for kv_head, q_ref in enumerate(queries):
        keys = kv_ref[pl.ds(start, window), pl.ds(kv_head * HEAD_SIZE, HEAD_SIZE)]
        values = kv_ref[pl.ds(start, window), pl.ds((kv_heads + kv_head) * HEAD_SIZE, HEAD_SIZE)]
        group = q_ref.shape[1] // HEAD_SIZE
        stacked = jnp.concatenate(
            [q_ref[:, h * HEAD_SIZE : (h + 1) * HEAD_SIZE] for h in range(group)], axis=0
        )
        scores = lax.dot_general(
            stacked, keys, (((1,), (1,)), ((), ())), preferred_element_type=jnp.float32
        )
        scores = scores + tall
        expo = jnp.exp(scores - jnp.max(scores, axis=-1, keepdims=True))
        weights = (expo * (1.0 / jnp.sum(expo, axis=-1, keepdims=True))).astype(jnp.bfloat16)
        mixed = jnp.dot(weights, values, preferred_element_type=jnp.float32).astype(jnp.bfloat16)
        for head in range(group):
            place = (kv_head * group + head) * HEAD_SIZE
            o_ref[:, place : place + HEAD_SIZE] = mixed[head * QUERY_BLOCK : (head + 1) * QUERY_BLOCK]


def attend(part, position, queries, all_kv):
    tokens, cols = queries[0].shape
    window = VISIBLE_SPAN + QUERY_BLOCK
    width = cols * len(queries)
    half = tokens // 2
    return pl.pallas_call(
        functools.partial(attend_kernel, part),
        grid=(half // QUERY_BLOCK,),
        in_specs=[pl.BlockSpec((QUERY_BLOCK, 1), lambda b: (2 * b + part, 0))]
        + [pl.BlockSpec((QUERY_BLOCK, cols), lambda b: (2 * b + part, 0)) for _ in queries]
        + [pl.BlockSpec(all_kv.shape, lambda b: (0, 0))],
        out_specs=pl.BlockSpec((QUERY_BLOCK, width), lambda b: (b, 0)),
        out_shape=jax.ShapeDtypeStruct((half, width), jnp.bfloat16),
        compiler_params=pltpu.CompilerParams(vmem_limit_bytes=20 * MIB),
        cost_estimate=lasting(0.1 if part else 14.5),
    )(position, *queries, all_kv)


def group_kernel(inner, planes, pairs, facts_ref, *refs):
    lefts, weights, outs = refs[:inner], refs[inner : -2 * len(pairs)], refs[-2 * len(pairs) :]
    place = facts_ref[planes]
    depth = lefts[0].shape[1]
    for n, weight_ref in enumerate(weights):
        total = None
        for m in range(inner):
            row = pl.multiple_of((place ^ m) * depth, depth)
            term = lax.dot_general(
                weight_ref[:, pl.ds(row, depth)],
                lefts[m][...],
                (((1,), (1,)), ((), ())),
                preferred_element_type=jnp.float32,
            )
            total = term if total is None else total + term
        total = total.astype(jnp.bfloat16)
        kept = facts_ref[planes + 1 + pairs[n // 2]]
        for out, which in zip(outs[n // 2 * 2 :], (kept, 1 - kept)):

            @pl.when(which == n % 2)
            def _():
                out[...] = total


def group_product(facts, attended, blocks, pairs):
    tokens, depth = attended[0].shape
    cols, rows = blocks[0].shape
    weights = [blocks[n] for pair in pairs for n in (pair, pair + len(blocks) // 2)]
    shape = jax.ShapeDtypeStruct((cols, tokens), jnp.bfloat16)
    outs = pl.pallas_call(
        functools.partial(group_kernel, len(attended), len(blocks), pairs),
        grid=(tokens // TOKEN_BLOCK,),
        in_specs=[pl.BlockSpec(memory_space=pltpu.SMEM)]
        + [pl.BlockSpec((TOKEN_BLOCK, depth), lambda b: (b, 0)) for _ in attended]
        + [pl.BlockSpec((cols, rows), lambda b: (0, 0)) for _ in weights],
        out_specs=[pl.BlockSpec((cols, TOKEN_BLOCK), lambda b: (0, b))] * len(weights),
        out_shape=[shape] * len(weights),
        compiler_params=pltpu.CompilerParams(vmem_limit_bytes=24 * MIB),
        cost_estimate=lasting(5.8 if pairs == (1,) else 0.1),
    )(facts, *attended, *weights)
    return outs[::2], outs[1::2]


def squares_kernel(*refs):
    total = None
    for ref in refs[:-1]:
        values = ref[...].astype(jnp.float32)
        term = jnp.sum(values * values, axis=0, keepdims=True)
        total = term if total is None else total + term
    refs[-1][...] = total


def squares_of(blocks):
    return pl.pallas_call(
        squares_kernel,
        out_shape=jax.ShapeDtypeStruct((1, blocks[0].shape[1]), jnp.float32),
        compiler_params=pltpu.CompilerParams(vmem_limit_bytes=8 * MIB),
    )(*blocks)


def finish_kernel(inner, planes, facts_ref, own_ref, other_ref, gain_ref, input_ref, *refs):
    o_ref, share_ref = refs[-2:]
    place = facts_ref[planes]
    pairs = planes // 2
    height = share_ref.shape[0] // (pairs * inner)
    pair = 0
    while pair < pairs:
        spread, refs = refs[:inner], refs[inner:]
        for m, ref in enumerate(spread):
            for n in range(ref.shape[0] // height):
                slot = facts_ref[planes + 1 + pairs + pair + n] * inner + (place ^ m)
                row = pl.multiple_of(slot * height, 16)
                share_ref[pl.ds(row, height), :] = ref[n * height : (n + 1) * height, :]
        pair += spread[0].shape[0] // height
    scale = lax.rsqrt((own_ref[...] + other_ref[...]) / MODEL_WIDTH + EPS)
    for col in range(0, share_ref.shape[0], HEAD_SIZE):
        span = slice(col, col + HEAD_SIZE)
        branch = (share_ref[span, :].astype(jnp.float32) * scale).T * gain_ref[:, span]
        o_ref[:, span] = (input_ref[:, span].astype(jnp.float32) + branch).astype(jnp.bfloat16)


def finish(part, planes, facts, own, other, gain, inputs, spread, so_far):
    rows, cols = inputs.shape
    step = own.shape[1]
    whole = lambda x: pl.BlockSpec(x.shape, lambda b: (0, 0))
    extra = [] if so_far is None else [so_far]
    gain = gain.reshape(1, cols)
    operands = [facts, own, other, gain, inputs, *spread, *extra]
    return pl.pallas_call(
        functools.partial(finish_kernel, INNER, planes),
        grid=(1,),
        in_specs=[pl.BlockSpec(memory_space=pltpu.SMEM), whole(own), whole(other), whole(gain)]
        + [pl.BlockSpec((step, cols), lambda b: (part, 0))]
        + [whole(block) for block in spread]
        + [pl.BlockSpec(memory_space=pl.ANY) for _ in extra],
        out_specs=pl.BlockSpec((step, cols), lambda b: (part, 0)),
        out_shape=jax.ShapeDtypeStruct((rows, cols), jnp.bfloat16),
        scratch_shapes=[pltpu.VMEM((cols, step), jnp.bfloat16)],
        input_output_aliases={len(operands) - 1: 0} if extra else {},
        compiler_params=pltpu.CompilerParams(vmem_limit_bytes=16 * MIB),
        cost_estimate=lasting(2.5),
    )(*operands)


def shuffle_start(weights, place):
    def cut(which):
        parts = []
        for core in range(2):
            cols = [w.shape[1] // INNER for w in weights]
            spans = [
                lax.dynamic_slice_in_dim(w, (which * 2 + core) * n, n, axis=1)
                for w, n in zip(weights, cols)
            ]
            parts.append(jnp.concatenate(spans, axis=1) if len(spans) > 1 else spans[0])
        return jnp.stack(parts)

    side = place // 2
    return cut(side), swap(cut(1 - side), 2)


def shuffle_end(mine, theirs, place):
    core = place % 2
    rows = in_order(place // 2 == 0, mine, theirs)
    keep = lax.dynamic_index_in_dim(rows, core, 1, keepdims=False)
    give = lax.dynamic_index_in_dim(rows, 1 - core, 1, keepdims=False)
    whole = in_order(core == 0, keep, swap(give, 1))
    return whole.transpose(1, 0, 2, 3).reshape(-1, whole.shape[-1])


def by_planes(
    inputs,
    in_gain,
    q_weight,
    key_matrix,
    value_matrix,
    q_gain,
    key_norm_gain,
    out_weight,
    post_gain,
    segment_ids,
    positions,
):
    tok_rows = inputs.shape[0]
    planes = lax.axis_size("z")
    place, plane, side = lax.axis_index("i"), lax.axis_index("z"), lax.axis_index("tp")
    plane_tokens = INNER * tok_rows
    per_side = planes // 2
    source = [(plane - d) % planes for d in range(planes)]
    kept, slots = [], []
    for d in range(per_side):
        near, opposite = source[d], source[d + per_side]
        kept.append(jnp.where(near // per_side == side, 0, 1))
        slots.append(jnp.where(kept[d] == 0, near, opposite) % per_side)
    facts = jnp.stack([*source, place, *kept, *slots]).astype(jnp.int32)

    kv_on_way = shuffle_start([key_matrix, value_matrix], place)
    out_rows = out_weight.T
    hops = {"o": [out_rows]}
    previous = []

    def hop(name, *others):
        block = hops[name][-1]
        hops[name].append(ring_step(after(block, *others) if others else block))
        previous.append(hops[name][-1])

    hop("o")
    values = after(inputs, kv_on_way[1]).astype(jnp.float32)
    squares = jnp.sum(values * values, axis=-1)
    scale = lax.rsqrt((squares + swap_tp(squares)) / MODEL_WIDTH + EPS)
    gain = lax.dynamic_slice_in_dim(in_gain, side * inputs.shape[1], inputs.shape[1])
    normed = (values * scale[:, None] * gain).astype(jnp.bfloat16)

    pos_x = in_order(place // 2 == 0, positions, swap(positions, 2))
    q_on_way = shuffle_start([after(q_weight, kv_on_way[1])], place)
    kv = shuffle_end(*kv_on_way, place)
    normed = lax.all_gather(after(normed, hops["o"][1], kv), ("i", "tp"), axis=0, tiled=False)
    normed = normed.reshape(INNER, 2, *inputs.shape)
    kv_half = kv.shape[1] // 2
    hops["k"], hops["v"] = [kv[:, :kv_half]], [kv[:, kv_half:]]
    pos = in_order(place % 2 == 0, pos_x, swap(pos_x, 1)).transpose(1, 0, 2).reshape(-1)
    hop("k")
    hop("v")
    q = shuffle_end(q_on_way[0], after(q_on_way[1], hops["k"][1]), place)
    q_half = q.shape[1] // 2
    hops["qa"], hops["qb"] = [q[:, :q_half]], [q[:, q_half:]]
    for name in ["k", "v"] * (planes - 2):
        hop(name, previous[-2])
    hop("qa", previous[-2])
    hop("qb", previous[-2])

    half = HEAD_SIZE // 2
    frequency = ROPE_BASE ** (-jnp.arange(half, dtype=jnp.float32) / half)
    angles = pos.astype(jnp.float32)[:, None] * frequency[None, :]
    turn = jnp.concatenate([jnp.cos(angles), jnp.sin(angles)], axis=1)

    own_kv = project(
        after(normed, turn),
        facts,
        [hops["k"], hops["v"]],
        1,
        key_norm_gain,
        turn,
    )
    for n in range(planes - 2):
        hop("qa", *[own_kv][:n])
        hop("qb", *[own_kv][:n])
    up = [(c, c + 1) for c in range(planes - 1)]
    halo = lax.ppermute(own_kv[plane_tokens - VISIBLE_SPAN :], "z", up)
    all_kv = jnp.concatenate([halo, own_kv], axis=0)
    for _ in range(planes - 3):
        hop("o", previous[-2])

    factor = (MODEL_WIDTH // QUERY_HEADS) ** (-0.5)
    queries = [
        project(after(normed, own_kv), facts, [hops[name]], 1, q_gain, turn, factor)
        for name in ("qa", "qb")
    ]

    own = [attend(0, pos[:, None], queries, all_kv)]
    own.append(attend(1, pos[:, None], [after(queries[0], own[0], hops["o"][planes - 2]), queries[1]], all_kv))
    hop("o", own[0])
    keeps, arrived = [], []
    for part in range(2):
        far = swap(own[part], 2)
        first = after(own[0], own[1]) if part == 0 else after(own[1], keeps[-1])
        across = after(far, *([own[1]] if part == 0 else [keeps[-1], arrived[0]]))
        attended = [first, swap(own[part], 1), far, swap(across, 1)]
        for pairs in [[n] for n in range(per_side)] if part == 0 else [range(per_side)]:
            kept_terms, given_terms = group_product(facts, attended, hops["o"], tuple(pairs))
            keeps += kept_terms
            arrived += [swap_tp(term) for term in given_terms]
            attended = [after(attended[0], keeps[-1]), *attended[1:]]

    def to_tokens(total):
        blocks = []
        for mask in range(INNER):
            at = (place ^ mask) * QUERY_BLOCK
            block = lax.dynamic_slice_in_dim(total, at, QUERY_BLOCK, axis=1)
            blocks.append(swap(block, mask) if mask else block)
        return blocks

    output = None
    for part in range(2):
        sums, spread = [], []
        for n in range(part * per_side, (part + 1) * per_side):
            theirs = after(arrived[n], *(keeps[-1:] if part == 0 else spread[-INNER + 1 :]))
            total = keeps[n].astype(jnp.float32) + theirs.astype(jnp.float32)
            sums.append(total.astype(jnp.bfloat16))
            if part == 1:
                spread += to_tokens(sums[-1])
        if part == 0:
            spread = to_tokens(jnp.concatenate(sums, axis=0))
        if output is not None:
            spread[-1] = after(spread[-1], output)
        squares = squares_of(spread)
        output = finish(
            part, planes, facts, squares, swap_tp(squares), post_gain, inputs, spread, output
        )
    return output


def from_behind(x, axis, by):
    size = lax.axis_size(axis)
    pairs = [(i, i + by) for i in range(size) if 0 <= i + by < size]
    return lax.ppermute(x, axis, pairs)


def block_scores(grouped, keys_block):
    return jnp.einsum("qhgd,khd->hgqk", grouped, keys_block, preferred_element_type=jnp.float32)


def block_mix(weights_block, values_block):
    return jnp.einsum(
        "hgqk,khd->qhgd", weights_block, values_block, preferred_element_type=jnp.float32
    )


def gather_features(inputs):
    if lax.axis_size("tp") != 2:
        return lax.all_gather(inputs, "tp", axis=1, tiled=True)
    other = lax.ppermute(inputs, "tp", [(0, 1), (1, 0)])
    first = lax.axis_index("tp") == 0
    return jnp.concatenate(
        [jnp.where(first, inputs, other), jnp.where(first, other, inputs)], axis=1
    )


def project_out(attended, out_full):
    if lax.axis_size("tp") != 2:
        partial_terms = jnp.dot(attended, out_full, preferred_element_type=jnp.float32)
        return lax.psum_scatter(
            partial_terms.astype(jnp.bfloat16), "tp", scatter_dimension=1, tiled=True
        ).astype(jnp.float32)
    here = lax.axis_index("tp")
    cols = out_full.shape[1] // 2

    def half(which):
        weight = lax.dynamic_slice_in_dim(out_full, which * cols, cols, axis=1)
        return jnp.dot(attended, weight, preferred_element_type=jnp.float32).astype(jnp.bfloat16)

    theirs = half(1 - here)
    arrived = lax.ppermute(theirs, "tp", [(0, 1), (1, 0)])
    return half(here).astype(jnp.float32) + arrived.astype(jnp.float32)


def by_devices(
    inputs,
    in_gain,
    q_weight,
    key_matrix,
    value_matrix,
    q_gain,
    key_norm_gain,
    out_weight,
    post_gain,
    segment_ids,
    positions,
):
    tok_rows = inputs.shape[0]
    q_cols = q_weight.shape[1]
    kv_cols = key_matrix.shape[1]
    stacked = jnp.concatenate([key_matrix, value_matrix, q_weight], axis=1)
    weights_full = lax.all_gather(stacked, "ctx", axis=0, tiled=True)
    out_full = lax.all_gather(out_weight, "ctx", axis=1, tiled=True)
    gathered = gather_features(inputs)
    normalized = rms_scale(gathered.astype(jnp.float32), in_gain).astype(jnp.bfloat16)
    raw = jnp.dot(normalized, weights_full, preferred_element_type=jnp.float32)
    k_raw = raw[:, :kv_cols]
    v_raw = raw[:, kv_cols : 2 * kv_cols]
    q_raw = raw[:, 2 * kv_cols :]
    q_heads = q_cols // HEAD_SIZE
    kv_heads = kv_cols // HEAD_SIZE
    turn = angles_of(positions, HEAD_SIZE // 2)
    query_heads_all = prepare_heads(
        q_raw, q_gain, turn, (MODEL_WIDTH // QUERY_HEADS) ** (-0.5)
    )
    keys_own = prepare_heads(k_raw, key_norm_gain, turn, 1.0)
    keys_own = keys_own.reshape(tok_rows, kv_heads, HEAD_SIZE)
    values_own = v_raw.reshape(tok_rows, kv_heads, HEAD_SIZE).astype(jnp.bfloat16)
    reach = (VISIBLE_SPAN - 1) // tok_rows + 1
    key_list = [keys_own]
    value_list = [values_own]
    segment_list = [segment_ids]
    for distance in range(1, reach + 1):
        far_keys, far_values, far_segments = from_behind(
            (keys_own, values_own, segment_ids), "ctx", distance
        )
        key_list.insert(0, far_keys)
        value_list.insert(0, far_values)
        segment_list.insert(0, far_segments)
    key_all = jnp.concatenate(key_list, axis=0)
    value_all = jnp.concatenate(value_list, axis=0)
    segment_all = jnp.concatenate(segment_list, axis=0)
    my_start = lax.axis_index("ctx") * tok_rows
    key_index = my_start - reach * tok_rows + jnp.arange((reach + 1) * tok_rows, dtype=jnp.int32)
    query_index = my_start + jnp.arange(tok_rows, dtype=jnp.int32)
    gap = query_index[:, None] - key_index[None, :]
    allowed = (
        (segment_ids[:, None] == segment_all[None, :])
        & (gap >= 0)
        & (gap < VISIBLE_SPAN)
        & (key_index[None, :] >= 0)
    )
    head_group = q_heads // kv_heads
    grouped = query_heads_all.reshape(tok_rows, kv_heads, head_group, HEAD_SIZE)
    scores = block_scores(grouped, key_all)
    scores = jnp.where(allowed[None, None], scores, MASKED)
    expo = jnp.exp(scores - jnp.max(scores, axis=-1, keepdims=True))
    weights = (expo / jnp.sum(expo, axis=-1, keepdims=True)).astype(jnp.bfloat16)
    mixed = block_mix(weights, value_all)
    attended = mixed.reshape(tok_rows, q_cols).astype(jnp.bfloat16)
    share = project_out(attended, out_full)
    squares = lax.psum(jnp.sum(share * share, axis=-1), "tp")
    branch = share * lax.rsqrt(squares[:, None] / MODEL_WIDTH + EPS) * post_gain
    return (inputs.astype(jnp.float32) + branch).astype(jnp.bfloat16)


def solution(mesh):
    ctx, tp = mesh.shape["ctx"], mesh.shape["tp"]
    whole_planes = tp == 2 and ctx % (2 * INNER) == 0
    if whole_planes:
        devices = mesh.devices.reshape(ctx // INNER, INNER, tp)
        mesh = jax.sharding.Mesh(devices, ("z", "i", "tp"))
    tokens = ("z", "i") if whole_planes else "ctx"
    return jax.shard_map(
        by_planes if whole_planes else by_devices,
        mesh=mesh,
        in_specs=(
            P(tokens, "tp"),
            P(),
            P(tokens, "tp"),
            P(tokens, "tp"),
            P(tokens, "tp"),
            P(),
            P(),
            P("tp", tokens),
            P("tp"),
            P(tokens),
            P(tokens),
        ),
        out_specs=P(tokens, "tp"),
        check_vma=False,
    )
```
